32 devices in a mesh: groups: 2 (over x), blk: 16 (over z, y, core).
Axes of the slice: x: 2, y: 2, z: 4, core: 2. Of those that a mesh axis runs over, the one named last changes fastest.
Arguments:
- ocean_state: float32 [2, 6, 256, 3600], P(None, None, ('groups', 'blk')), parts along dimension 2, may hold values from -6 to 6
- kappa_h: float32 [128, 3600], P('blk'), may hold values from 0.02 to 0.15
- kappa_v: float32 [6], replicated, may hold values from 0.02 to 0.15
- wet_depth: int32 [128, 3600], P('blk'), may hold values from 0 to 6
- coupling: float32 [12, 12], replicated, may hold values from -8 to 8
- dest_of_block: int32 [3600, 1], P('blk'), may hold values from 0 to 15; in each aligned block of 225 rows (0 to 224, 225 to 449, ...) at most 22 rows name the same one
- tile_of_block: int32 [3600], P('blk'), may hold values from 0 to 7
- remap_weights: bfloat16 [3600, 128, 128], P('blk'), may hold values from 0.0077819824 to 0.0625
Outputs:
- ocean_next: float32 [2, 6, 256, 3600], P(None, None, ('groups', 'blk')), parts along dimension 2
- atm_fields: float32 [12, 32768], P(None, ('groups', 'blk')), parts along dimension 1
The draws below stay inside these ranges and needn't reach their ends.
There are 2 independent parts, one for each index of `groups`. The reference program is written for one: setup_inputs(seed, part) draws one part's arguments, and reference() takes and returns one part's arrays. A program takes and returns all parts, laid end to end along the dimension named above; an argument that names none is the same for every part. Nothing has to cross between parts.
Inputs may be any that keep to these rules, and one draw needn't show every extreme that they name: `dest_of_block`: among the 225 blocks of one device at most 22 name the same owner, and some owner gets exactly 22 of them.
All inputs are finite; a program needn't handle non-finite values.
Results may differ from the reference program's by a relative error of at most 0.0029.
Values sent between devices are 32-bit elements; how exact they have to be, the bound alone decides.
A program may use at most 64 MiB of HBM per device.

```python
import math
import jax
import jax.numpy as jnp
import numpy as np
from jax import lax

NLON = 3600
NZ = 6
FIELDS = 12
CB = 128
AT = 128
NTILE = 8
NBD = 225
CAP = 22
NY = 128
BLOCKS = 3600
ATM = 16384
N_BLK = 16


def set_ends(values, key, low, high):
    longest = values.shape.index(max(values.shape))
    spots = []
    for shift in (0, 1):
        where = [jax.random.randint(jax.random.fold_in(key, axis), (), 0, length) for axis, length in enumerate(values.shape)]
        where[longest] = (where[longest] + shift) % values.shape[longest]
        spots.append(tuple(where))
    return values.at[spots[0]].set(low).at[spots[1]].set(high)


def steps_of(stream_key, extent, cuts, least, top_value):
    level = 1.0
    for position, shards_of in cuts:
        steps = jax.random.uniform(jax.random.fold_in(jax.random.fold_in(stream_key, 6), position), (shards_of,), jnp.float32, least / len(cuts), top_value / len(cuts))
        level = level * jnp.repeat(jnp.exp(steps), extent[position] // shards_of).reshape((-1,) + (1,) * (len(extent) - 1 - position))
    return level


def shared_out(key, own, number, rows, amount, top, most, skew):
    sequence = jax.random.permutation(key, amount)
    heavy_load, common = portions_of(amount, rows * top, most, skew, True), portions_of(amount, rows * top, most, skew, False)
    places = jnp.arange(amount)

    def named(sizes, turn):
        used = int((sizes > 0).sum())
        fixed = max(1, used // 4)
        shifted = fixed + (places - fixed + turn * (used - fixed)) % max(1, amount - fixed)
        return jnp.zeros((amount,), jnp.int32).at[sequence[jnp.where(places < fixed, places, shifted)]].set(jnp.asarray(sizes, jnp.int32))

    sizes = jnp.where(number % 4 == 0, named(heavy_load, number // 4), named(common, number - number // 4 - 1))
    mixed = jax.random.permutation(jax.random.fold_in(own, 3), amount)
    donor, sink = mixed[0:amount // 2 * 2:2], mixed[1:amount // 2 * 2:2]
    slack = jnp.minimum(sizes[donor] - 1, most - sizes[sink]) // 2
    slack = jnp.where((donor == sequence[0]) | (sink == sequence[0]) | (sizes[sink] == 0), 0, jnp.maximum(slack, 0))
    shifted = jax.random.randint(jax.random.fold_in(own, 4), (amount // 2,), 0, 1 << 20) % (slack + 1)
    sizes = sizes.at[donor].add(-shifted).at[sink].add(shifted)
    members = jnp.searchsorted(jnp.cumsum(sizes), jnp.arange(rows * top), side="right").astype(jnp.int32)
    listing = members.reshape(top, rows).T
    listing = listing[jax.random.permutation(jax.random.fold_in(own, 1), rows)]
    turn = jax.random.randint(jax.random.fold_in(own, 2), (rows, 1), 0, top)
    return jnp.take_along_axis(listing, (jnp.arange(top)[None, :] + turn) % top, axis=1)


def portions_of(count, total, reach, lean, full):
    loads = [(1 << 20) // math.isqrt(rank ** lean) + 1 for rank in range(1, count + 1)]
    largest = reach if full else min(reach, max(-(-total // count), total * loads[0] // sum(loads)))
    least = 1 if total - largest >= count - 1 else 0
    counts, surplus = [largest] + [least] * (count - 1), total - largest - least * (count - 1)
    while surplus > 0:
        candidates = [i for i in range(1, count) if counts[i] < largest] or [i for i in range(1, count) if counts[i] < reach]
        whole, left = sum([loads[i] for i in candidates]), surplus
        for i in candidates:
            extra = min(reach - counts[i], max(1, left * loads[i] // whole), surplus)
            counts[i] = counts[i] + extra
            surplus = surplus - extra
    return np.array(counts)


def normal_values(key, shape, spread, most, split=(), held_as=jnp.bfloat16):
    loudness = steps_of(key, shape, split, -0.22, 0.18) if split else 1.0
    drawn = jax.random.normal(key, shape, jnp.float32) * spread * loudness
    return jnp.minimum(jnp.maximum(drawn, -most), most).astype(held_as)


def setup_inputs(seed: int = 0, part: int = 0) -> dict:
    streams_of = jax.random.split(jax.random.key(seed), 9)
    part_keys = jax.random.split(jax.random.fold_in(streams_of[8], part), 9)
    ocean_state = normal_values(part_keys[0], (2, NZ, NY, NLON), 1.0, 6.0, ((2, 16),), jnp.float32)
    kappa_h = jnp.clip(jnp.exp(math.log(0.15) - 2.014903 * jax.random.uniform(streams_of[1], (NY, NLON), jnp.float32) ** steps_of(streams_of[1], (NY, NLON), ((0, 16),), -0.2, 0.2)), 0.02, 0.15)
    kappa_v = jnp.clip(jnp.exp(jax.random.uniform(streams_of[2], (NZ,), jnp.float32, math.log(0.02), math.log(0.15))), 0.02, 0.15)
    wet_depth = set_ends(jax.random.randint(streams_of[3], (NY, NLON), 0, NZ + 1), jax.random.fold_in(streams_of[3], 1), 0, NZ).astype(jnp.int32)
    coupling = normal_values(streams_of[4], (FIELDS, 2 * NZ), 2.0, 8.0, (), jnp.float32)
    dest_of_block_keys = jax.random.split(jax.random.fold_in(streams_of[5], 1), BLOCKS // NBD)
    dest_of_block_turns = jax.random.permutation(jax.random.fold_in(streams_of[5], 3), BLOCKS // NBD)
    dest_of_block = jax.vmap(lambda own, number: shared_out(jax.random.fold_in(streams_of[5], 2), own, number, NBD, N_BLK, 1, CAP, 2))(dest_of_block_keys, dest_of_block_turns).reshape((BLOCKS, 1))
    tile_of_block = set_ends(jax.random.randint(streams_of[6], (BLOCKS,), 0, NTILE), jax.random.fold_in(streams_of[6], 1), 0, NTILE - 1).astype(jnp.int32)
    remap_weights = jnp.clip(jnp.exp(math.log(0.0625) - 2.0833554 * jax.random.uniform(streams_of[7], (BLOCKS, CB, AT), jnp.float32) ** steps_of(streams_of[7], (BLOCKS, CB, AT), ((0, 16),), -0.2, 0.2)), 0.0077819824, 0.0625).astype(jnp.bfloat16)
    return {"ocean_state": ocean_state, "kappa_h": kappa_h, "kappa_v": kappa_v, "wet_depth": wet_depth, "coupling": coupling, "dest_of_block": dest_of_block, "tile_of_block": tile_of_block, "remap_weights": remap_weights}


def conductance(kappa_h, wet_depth):
    levels = jnp.arange(NZ, dtype=jnp.int32)[:, None, None]
    return jnp.where(levels < wet_depth[None], kappa_h[None], jnp.zeros_like(kappa_h)[None])

def mix_step(extended, conduct, kappa_v):
    centre = extended[:, :, 1:-1]
    conduct_mid = conduct[:, 1:-1]
    east_face = jnp.sqrt(conduct_mid * jnp.roll(conduct_mid, -1, axis=-1))
    east_flux = east_face * (jnp.roll(centre, -1, axis=-1) - centre)
    change = east_flux - jnp.roll(east_flux, 1, axis=-1)
    north_face = jnp.sqrt(conduct[:, 1:] * conduct[:, :-1])
    north_flux = north_face * (extended[:, :, 1:] - extended[:, :, :-1])
    change = change + north_flux[:, :, 1:] - north_flux[:, :, :-1]
    wet_mask = jnp.where(conduct_mid > 0.0, jnp.ones_like(conduct_mid), jnp.zeros_like(conduct_mid))
    vert_coef = kappa_v[:-1, None, None] * wet_mask[:-1] * wet_mask[1:]
    vert_flux = vert_coef * (centre[:, 1:] - centre[:, :-1])
    zero_level = jnp.zeros_like(centre[:, :1])
    change = change + jnp.concatenate([vert_flux, zero_level], axis=1) - jnp.concatenate([zero_level, vert_flux], axis=1)
    return centre + change

def block_products(pair):
    return jnp.einsum('brc,bca->bra', pair[0].astype(jnp.float32), pair[1].astype(jnp.float32), precision=lax.Precision.HIGHEST)

def reference(ocean_state, kappa_h, kappa_v, wet_depth, coupling, dest_of_block, tile_of_block, remap_weights):
    conduct = conductance(kappa_h, wet_depth)
    conduct_ext = jnp.pad(conduct, ((0, 0), (1, 1), (0, 0)))
    row_pad = ((0, 0), (0, 0), (1, 1), (0, 0))
    ocean_mid = mix_step(jnp.pad(ocean_state, row_pad), conduct_ext, kappa_v)
    ocean_next = mix_step(jnp.pad(ocean_mid, row_pad), conduct_ext, kappa_v)
    profile = ocean_next.reshape(2 * NZ, NY * NLON)
    fields = jnp.dot(coupling, profile, precision=lax.Precision.HIGHEST)
    sea_mask = jnp.where(wet_depth > 0, jnp.ones_like(kappa_h), jnp.zeros_like(kappa_h)).reshape(-1)
    surface = jnp.concatenate([fields * sea_mask[None], sea_mask[None]], axis=0).astype(jnp.bfloat16)
    blocks = surface.reshape(FIELDS + 1, BLOCKS, CB).transpose(1, 0, 2)
    grouped = blocks.reshape(N_BLK, NBD, FIELDS + 1, CB)
    weight_groups = remap_weights.reshape(N_BLK, NBD, CB, AT)
    partial_value = lax.map(block_products, (grouped, weight_groups)).reshape(BLOCKS, FIELDS + 1, AT)
    segment_key = (dest_of_block[:, 0] * NTILE + tile_of_block).astype(jnp.int32)
    tile_sum = jax.ops.segment_sum(partial_value, segment_key, num_segments=N_BLK * NTILE)
    numerator = tile_sum[:, :FIELDS]
    denominator = jnp.maximum(tile_sum[:, FIELDS], 1.0)
    atm_fields = (numerator / denominator[:, None]).transpose(1, 0, 2).reshape(FIELDS, ATM)
    return (ocean_next, atm_fields)
```

```python
import functools

import jax
import jax.numpy as jnp
from jax import lax
from jax.experimental import pallas as pl
from jax.experimental.pallas import tpu as pltpu
from jax.sharding import PartitionSpec as P

NZ = 6
FIELDS = 12
CB = 128
AT = 128
NTILE = 8
ROWS = 8
LANES = 128
WIDE = 16
HIGH = lax.Precision.HIGHEST


def lane_pair(cur, before, after, lane):
    east = pltpu.roll(jnp.where(lane == 0, after, cur), LANES - 1, 1)
    west = pltpu.roll(jnp.where(lane == LANES - 1, before, cur), 1, 1)
    return east, west


def row_pair(cur, other, sub):
    up = pltpu.roll(jnp.where(sub == ROWS - 1, other, cur), 1, 0)
    down = pltpu.roll(jnp.where(sub == 0, other, cur), ROWS - 1, 0)
    return up, down


def faces(kap, wet, other_kap, other_wet, lane, sub):
    cur, wcur = kap[0], wet[0]
    nbk = lane_pair(*kap, lane) + row_pair(cur, other_kap, sub)
    nbw = lane_pair(*wet, lane) + row_pair(wcur, other_wet, sub)
    return [(jnp.sqrt(cur * k), jnp.minimum(wcur, w)) for k, w in zip(nbk, nbw)]


def mixed(tiles, others, face, wet, kv, lane, sub):
    out = [[None] * NZ for _ in range(2)]
    for l in range(NZ):
        coef = [jnp.where(l < depth, root, 0.0) for root, depth in face]
        below = jnp.where(l + 1 < wet, kv[l], 0.0) if l + 1 < NZ else None
        above = jnp.where(l < wet, kv[l - 1], 0.0) if l > 0 else None
        for c in range(2):
            cur = tiles[c][l][0]
            near = lane_pair(*tiles[c][l], lane) + row_pair(cur, others[c][l], sub)
            change = coef[0] * (near[0] - cur)
            for a, v in zip(coef[1:], near[1:]):
                change = change + a * (v - cur)
            if below is not None:
                change = change + below * (tiles[c][l + 1][0] - cur)
            if above is not None:
                change = change + above * (tiles[c][l - 1][0] - cur)
            out[c][l] = cur + change
    return out


def local_kernel(
    u_ref, kap_ref, wet_ref, halo_ref, kv_ref, coup_ref, dest_ref, tile_ref, w_hbm,
    next_ref, sums_ref,
    full, mid, surf, blocks, acc, weights, w_sem,
):
    length = u_ref.shape[-1]
    count = w_hbm.shape[0]
    tiles = full.shape[-1] // LANES
    last = tiles - 1
    rem = length - last * LANES
    cut = last * LANES
    fetch = pltpu.make_async_copy(w_hbm, weights, w_sem)
    fetch.start()

    lane = lax.broadcasted_iota(jnp.int32, (ROWS, LANES), 1)
    sub = lax.broadcasted_iota(jnp.int32, (ROWS, LANES), 0)
    kv = [kv_ref[l] for l in range(NZ)]

    def place(side, q, value):
        full[side, q, :, 0:cut] = value[:, 0:cut]
        tail = jnp.concatenate(
            [value[:, cut:length], jnp.zeros((ROWS, LANES - rem), jnp.float32)], axis=1
        )
        half = rem + (LANES - rem) // 2
        tail = jnp.where(
            lane < rem,
            tail,
            jnp.where(
                lane < half,
                pltpu.roll(value[:, 0:LANES], rem, 1),
                pltpu.roll(tail, LANES - rem, 1),
            ),
        )
        full[side, q, :, cut:] = tail

    for c in range(2):
        for l in range(NZ):
            place(0, c * NZ + l, u_ref[c, l])
    place(0, 12, kap_ref[...])
    place(0, 13, wet_ref[...].astype(jnp.float32))
    for q in range(14):
        place(1, q, halo_ref[q])
    acc[...] = jnp.zeros_like(acc)

    def columns(t):
        def at(i):
            return pl.ds(pl.multiple_of(i * LANES, LANES), LANES)

        return [at(t), at(lax.rem(t + last, tiles)), at(lax.rem(t + 1, tiles))]

    def first(t, carry):
        cols = columns(t)
        get = lambda side, q: [full[side, q, :, s] for s in cols]
        state = [[[get(side, c * NZ + l) for l in range(NZ)] for c in range(2)] for side in range(2)]
        kap = [get(side, 12) for side in range(2)]
        wet = [get(side, 13) for side in range(2)]
        for side in range(2):
            o = 1 - side
            face = faces(kap[side], wet[side], kap[o][0], wet[o][0], lane, sub)
            others = [[state[o][c][l][0] for l in range(NZ)] for c in range(2)]
            new = mixed(state[side], others, face, wet[side][0], kv, lane, sub)
            for c in range(2):
                for l in range(NZ):
                    mid[side, c * NZ + l, :, cols[0]] = new[c][l]
        return carry

    lax.fori_loop(0, tiles, first, 0)

    big = ROWS * WIDE
    inner = (FIELDS + 1) * ROWS
    r0 = lax.broadcasted_iota(jnp.int32, (big, FIELDS), 0)
    r1 = lax.broadcasted_iota(jnp.int32, (big, FIELDS), 1)
    pick_f = jnp.where(lax.rem(r0, WIDE) == r1, 1.0, 0.0)
    q0 = lax.broadcasted_iota(jnp.int32, (FIELDS, inner), 0)
    q1 = lax.broadcasted_iota(jnp.int32, (FIELDS, inner), 1)
    pick_q = jnp.where(q1 // ROWS == q0, 1.0, 0.0)
    spread = jnp.dot(
        jnp.dot(pick_f, coup_ref[...], precision=HIGH, preferred_element_type=jnp.float32),
        pick_q, precision=HIGH, preferred_element_type=jnp.float32,
    )
    m0 = lax.broadcasted_iota(jnp.int32, (big, inner), 0)
    m1 = lax.broadcasted_iota(jnp.int32, (big, inner), 1)
    same = (m0 // WIDE) == lax.rem(m1, ROWS)
    sea_entry = (lax.rem(m0, WIDE) == FIELDS) & (m1 // ROWS == FIELDS)
    spread = jnp.where(same, jnp.where(sea_entry, 1.0, spread), 0.0)

    def second(t):
        cols = columns(t)
        get = lambda ref, side, q: [ref[side, q, :, s] for s in cols]
        state = [[get(mid, 0, c * NZ + l) for l in range(NZ)] for c in range(2)]
        others = [[mid[1, c * NZ + l, :, cols[0]] for l in range(NZ)] for c in range(2)]
        kap, wet = get(full, 0, 12), get(full, 0, 13)
        face = faces(kap, wet, full[1, 12, :, cols[0]], full[1, 13, :, cols[0]], lane, sub)
        new = mixed(state, others, face, wet[0], kv, lane, sub)
        sea = jnp.where(wet[0] > 0.0, 1.0, 0.0)
        rows = [new[c][l] * sea for c in range(2) for l in range(NZ)] + [sea]
        surf[:, cols[0]] = jnp.dot(
            spread, jnp.concatenate(rows, axis=0), precision=HIGH,
            preferred_element_type=jnp.float32,
        )
        return new, cols[0]

    def second_loop(t, carry):
        new, here = second(t)
        for c in range(2):
            for l in range(NZ):
                next_ref[c, l, :, here] = new[c][l]
        return carry

    lax.fori_loop(0, last, second_loop, 0)
    new, _ = second(last)
    for c in range(2):
        for l in range(NZ):
            next_ref[c, l, :, cut:length] = new[c][l][:, 0:rem]

    wlane = lax.broadcasted_iota(jnp.int32, (WIDE, LANES), 1)

    def shifted(j, cur, before):
        shift = rem * j
        if shift == 0:
            return cur
        return pltpu.roll(jnp.where(wlane < LANES - shift, cur, before), shift, 1)

    def align(t, carry):
        here = pl.ds(pl.multiple_of(t * LANES, LANES), LANES)
        prev = pl.ds(pl.multiple_of((t - 1) * LANES, LANES), LANES)
        for j in range(ROWS):
            rows = pl.ds(j * WIDE, WIDE)
            value = shifted(j, surf[rows, here], surf[rows, prev])
            blocks[last * j + t] = value.astype(jnp.bfloat16)
        return carry

    lax.fori_loop(1, last, align, 0)
    for j in range(ROWS + 1):
        if j > 0:
            rows = pl.ds((j - 1) * WIDE, WIDE)
            tail = shifted(j - 1, surf[rows, cut:cut + LANES], surf[rows, cut - LANES:cut])
        if j < ROWS:
            head = surf[pl.ds(j * WIDE, WIDE), 0:LANES]
            if j > 0:
                head = jnp.where(wlane >= rem * j, pltpu.roll(head, rem * j, 1), tail)
        else:
            head = tail
        blocks[last * j] = head.astype(jnp.bfloat16)

    fetch.wait()

    def product(g, carry):
        value = jnp.dot(blocks[g], weights[g], preferred_element_type=jnp.float32)
        seg = dest_ref[g] * NTILE + tile_ref[g]
        here = pl.ds(pl.multiple_of(seg * WIDE, WIDE), WIDE)
        acc[here, :] = acc[here, :] + value
        return carry

    lax.fori_loop(0, count, product, 0, unroll=9)

    owners = sums_ref.shape[0]
    quarter = owners // 4

    def deliver(d, carry):
        slot = lax.rem(d, 4)
        slot = (lax.rem(slot, 2) * 2 + slot // 2) * quarter + d // 4
        for r in range(FIELDS + 1):
            sums_ref[slot, r] = acc[pl.ds(d * (NTILE * WIDE) + r, NTILE, stride=WIDE), :]
        return carry

    lax.fori_loop(0, owners, deliver, 0)


def local_part(u, kap, wet, halo, kv, coup, dest, tile, weights, owners):
    length = u.shape[-1]
    pad = -(-length // LANES) * LANES
    count = weights.shape[0]
    vmem = pl.BlockSpec(memory_space=pltpu.VMEM)
    smem = pl.BlockSpec(memory_space=pltpu.SMEM)
    return pl.pallas_call(
        local_kernel,
        name="mix_and_remap",
        out_shape=(
            jax.ShapeDtypeStruct(u.shape, jnp.float32),
            jax.ShapeDtypeStruct((owners, FIELDS + 1, NTILE, AT), jnp.float32),
        ),
        in_specs=[vmem, vmem, vmem, vmem, smem, vmem, smem, smem, pl.BlockSpec(memory_space=pl.ANY)],
        out_specs=(vmem, vmem),
        scratch_shapes=[
            pltpu.VMEM((2, 14, ROWS, pad), jnp.float32),
            pltpu.VMEM((2, 12, ROWS, pad), jnp.float32),
            pltpu.VMEM((ROWS * WIDE, pad), jnp.float32),
            pltpu.VMEM((count, WIDE, CB), jnp.bfloat16),
            pltpu.VMEM((owners * NTILE * WIDE, AT), jnp.float32),
            pltpu.VMEM(weights.shape, jnp.bfloat16),
            pltpu.SemaphoreType.DMA,
        ],
        compiler_params=pltpu.CompilerParams(vmem_limit_bytes=44 * 2**20),
    )(u, kap, wet, halo, kv, coup, dest, tile, weights)


PARTS = ((0, 7), (7, 13))


def owner_kernel(n, sums_ref, out_ref, sum1, sum2, got1, got2, got3, ratio, send, recv):
    me = lax.axis_index("blk")
    quarter = n // 4
    core, side, q = lax.rem(me, 2), lax.rem(me // 2, 2), me // 4
    mate1 = me + 1 - 2 * core
    mate2 = me + 2 - 4 * side
    line = [(lax.rem(q + k, quarter)) * 4 + lax.rem(me, 4) for k in range(1, quarter)]

    barrier = pltpu.get_barrier_semaphore()
    for other in [mate1, mate2] + line:
        pl.semaphore_signal(
            barrier, inc=1, device_id={"blk": other}, device_id_type=pl.DeviceIdType.MESH
        )
    pl.semaphore_wait(barrier, 1 + quarter)

    def copy(src, dst, index, other):
        return pltpu.make_async_remote_copy(
            src_ref=src, dst_ref=dst, send_sem=send.at[index], recv_sem=recv.at[index],
            device_id={"blk": other}, device_id_type=pl.DeviceIdType.MESH,
        )

    np_ = len(PARTS)
    ones, twos, threes = [], [], []
    for i, (a, b) in enumerate(PARTS):
        rows = pl.ds(a, b - a)
        ones.append(copy(sums_ref.at[1 - core, :, :, rows], got1.at[:, :, rows], i, mate1))
        ones[-1].start()
    for i, (a, b) in enumerate(PARTS):
        rows = pl.ds(a, b - a)
        ones[i].wait_recv()
        sum1[:, :, rows] = sums_ref[core, :, :, rows] + got1[:, :, rows]
        twos.append(copy(sum1.at[1 - side, :, rows], got2.at[:, rows], np_ + i, mate2))
        twos[-1].start()
    for i, (a, b) in enumerate(PARTS):
        rows = pl.ds(a, b - a)
        twos[i].wait_recv()
        sum2[:, rows] = sum1[side, :, rows] + got2[:, rows]
        threes.append([])
        for k in range(1, quarter):
            to = lax.rem(q + k, quarter)
            threes[i].append(
                copy(sum2.at[to, rows], got3.at[k - 1, rows], 2 * np_ + (k - 1) * np_ + i, line[k - 1])
            )
            threes[i][-1].start()
    total = []
    for i, (a, b) in enumerate(PARTS):
        rows = pl.ds(a, b - a)
        value = sum2[q, rows]
        for k in range(1, quarter):
            threes[i][k - 1].wait_recv()
            value = value + got3[k - 1, rows]
        total.append(value)
    total = jnp.concatenate(total, axis=0)
    below = jnp.maximum(total[FIELDS], 1.0)
    for f in range(FIELDS):
        ratio[f * NTILE:(f + 1) * NTILE, :] = total[f] / below
    for t in range(NTILE):
        out_ref[:, t * AT:(t + 1) * AT] = ratio[pl.ds(t, FIELDS, stride=NTILE), :]
    for group in [ones, twos] + threes:
        for one in group:
            one.wait_send()


def owner_part(sums):
    n = sums.shape[0]
    quarter = n // 4
    block = sums.shape[1:]
    slots = (2 + quarter) * len(PARTS)
    vmem = pl.BlockSpec(memory_space=pltpu.VMEM)
    return pl.pallas_call(
        functools.partial(owner_kernel, n),
        name="owner_sums",
        out_shape=jax.ShapeDtypeStruct((FIELDS, NTILE * AT), jnp.float32),
        in_specs=[vmem],
        out_specs=vmem,
        scratch_shapes=[
            pltpu.VMEM((2, quarter) + block, jnp.float32),
            pltpu.VMEM((quarter,) + block, jnp.float32),
            pltpu.VMEM((2, quarter) + block, jnp.float32),
            pltpu.VMEM((quarter,) + block, jnp.float32),
            pltpu.VMEM((max(1, quarter - 1),) + block, jnp.float32),
            pltpu.VMEM((FIELDS * NTILE, AT), jnp.float32),
            pltpu.SemaphoreType.DMA((slots,)),
            pltpu.SemaphoreType.DMA((slots,)),
        ],
        compiler_params=pltpu.CompilerParams(
            collective_id=0, has_side_effects=True, vmem_limit_bytes=40 * 2**20
        ),
    )(sums.reshape((2, 2, quarter) + block))


def body(
    ocean_state, kappa_h, kappa_v, wet_depth, coupling, dest_of_block, tile_of_block, remap_weights
):
    size = lax.axis_size("blk")
    length = ocean_state.shape[-1]
    stacked = jnp.concatenate(
        [
            ocean_state.reshape(2 * NZ, ROWS, length),
            kappa_h[None],
            wet_depth.astype(jnp.float32)[None],
        ],
        axis=0,
    )
    up = [(i, i + 1) for i in range(size - 1)]
    down = [(i + 1, i) for i in range(size - 1)]
    before = lax.ppermute(stacked[:, ROWS - 2:], "blk", up)
    after = lax.ppermute(stacked[:, :2], "blk", down)
    zeros = jnp.zeros((2 * NZ + 2, ROWS - 4, length), jnp.float32)
    halo = jnp.concatenate([after, zeros, before], axis=1)
    ocean_next, sums = local_part(
        ocean_state, kappa_h, wet_depth, halo, kappa_v, coupling,
        dest_of_block.reshape(-1), tile_of_block, remap_weights, size,
    )
    return ocean_next, owner_part(sums)


def solution(mesh):
    return jax.shard_map(
        body,
        mesh=mesh,
        in_specs=(
            P(None, None, ("groups", "blk"), None),
            P("blk", None),
            P(),
            P("blk", None),
            P(),
            P("blk", None),
            P("blk"),
            P("blk", None, None),
        ),
        out_specs=(P(None, None, ("groups", "blk"), None), P(None, ("groups", "blk"))),
        check_vma=False,
    )
```

```python
import functools

import jax
import jax.numpy as jnp
from jax import lax
from jax.experimental import pallas as pl
from jax.experimental.pallas import tpu as pltpu
from jax.sharding import PartitionSpec as P

NZ = 6
FIELDS = 12
CB = 128
AT = 128
NTILE = 8
ROWS = 8
LANES = 128
WIDE = 16
HIGH = lax.Precision.HIGHEST


def lane_pair(cur, before, after, lane):
    east = pltpu.roll(jnp.where(lane == 0, after, cur), LANES - 1, 1)
    west = pltpu.roll(jnp.where(lane == LANES - 1, before, cur), 1, 1)
    return east, west


def row_pair(cur, other, sub):
    up = pltpu.roll(jnp.where(sub == ROWS - 1, other, cur), 1, 0)
    down = pltpu.roll(jnp.where(sub == 0, other, cur), ROWS - 1, 0)
    return up, down


def faces(kap, wet, other_kap, other_wet, lane, sub):
    cur, wcur = kap[0], wet[0]
    nbk = lane_pair(*kap, lane) + row_pair(cur, other_kap, sub)
    nbw = lane_pair(*wet, lane) + row_pair(wcur, other_wet, sub)
    return [(jnp.sqrt(cur * k), jnp.minimum(wcur, w)) for k, w in zip(nbk, nbw)]


def halves(x):
    hi = x.astype(jnp.bfloat16)
    return hi, (x - hi.astype(jnp.float32)).astype(jnp.bfloat16)


def mixed(tiles, others, face, wet, kv, lane, sub):
    out = [[None] * NZ for _ in range(2)]
    for l in range(NZ):
        coef = [jnp.where(l < depth, root, 0.0) for root, depth in face]
        below = jnp.where(l + 1 < wet, kv[l], 0.0) if l + 1 < NZ else None
        above = jnp.where(l < wet, kv[l - 1], 0.0) if l > 0 else None
        for c in range(2):
            cur = tiles[c][l][0]
            near = lane_pair(*tiles[c][l], lane) + row_pair(cur, others[c][l], sub)
            change = coef[0] * (near[0] - cur)
            for a, v in zip(coef[1:], near[1:]):
                change = change + a * (v - cur)
            if below is not None:
                change = change + below * (tiles[c][l + 1][0] - cur)
            if above is not None:
                change = change + above * (tiles[c][l - 1][0] - cur)
            out[c][l] = cur + change
    return out


def local_kernel(
    u_ref, kap_ref, wet_ref, halo_u, halo_kap, halo_wet, kv_ref, coup_ref, dest_ref, tile_ref, w_hbm,
    next_ref, sums_ref,
    full, mid, surf, blocks, acc, weights, w_sem,
):
    length = u_ref.shape[-1]
    count = w_hbm.shape[0]
    tiles = full.shape[-1] // LANES
    last = tiles - 1
    rem = length - last * LANES
    cut = last * LANES
    fetch = pltpu.make_async_copy(w_hbm, weights, w_sem)
    fetch.start()

    lane = lax.broadcasted_iota(jnp.int32, (ROWS, LANES), 1)
    sub = lax.broadcasted_iota(jnp.int32, (ROWS, LANES), 0)
    kv = [kv_ref[l] for l in range(NZ)]

    def place(side, q, value):
        full[side, q, :, 0:cut] = value[:, 0:cut]
        tail = jnp.concatenate(
            [value[:, cut:length], jnp.zeros((ROWS, LANES - rem), jnp.float32)], axis=1
        )
        half = rem + (LANES - rem) // 2
        tail = jnp.where(
            lane < rem,
            tail,
            jnp.where(
                lane < half,
                pltpu.roll(value[:, 0:LANES], rem, 1),
                pltpu.roll(tail, LANES - rem, 1),
            ),
        )
        full[side, q, :, cut:] = tail

    for c in range(2):
        for l in range(NZ):
            place(0, c * NZ + l, u_ref[c, l])
    place(0, 12, kap_ref[...])
    place(0, 13, wet_ref[...].astype(jnp.float32))
    for c in range(2):
        for l in range(NZ):
            place(1, c * NZ + l, halo_u[c, l])
    place(1, 12, halo_kap[...])
    place(1, 13, halo_wet[...].astype(jnp.float32))
    acc[...] = jnp.zeros_like(acc)

    def columns(t):
        def at(i):
            return pl.ds(pl.multiple_of(i * LANES, LANES), LANES)

        return [at(t), at(lax.rem(t + last, tiles)), at(lax.rem(t + 1, tiles))]

    def first(t, carry):
        cols = columns(t)
        get = lambda side, q: [full[side, q, :, s] for s in cols]
        state = [[[get(side, c * NZ + l) for l in range(NZ)] for c in range(2)] for side in range(2)]
        kap = [get(side, 12) for side in range(2)]
        wet = [get(side, 13) for side in range(2)]
        for side in range(2):
            o = 1 - side
            face = faces(kap[side], wet[side], kap[o][0], wet[o][0], lane, sub)
            others = [[state[o][c][l][0] for l in range(NZ)] for c in range(2)]
            new = mixed(state[side], others, face, wet[side][0], kv, lane, sub)
            for c in range(2):
                for l in range(NZ):
                    mid[side, c * NZ + l, :, cols[0]] = new[c][l]
        return carry

    lax.fori_loop(0, tiles, first, 0)

    big = ROWS * WIDE
    inner = (FIELDS + 1) * ROWS
    r0 = lax.broadcasted_iota(jnp.int32, (big, FIELDS), 0)
    r1 = lax.broadcasted_iota(jnp.int32, (big, FIELDS), 1)
    pick_f = jnp.where(lax.rem(r0, WIDE) == r1, 1.0, 0.0)
    q0 = lax.broadcasted_iota(jnp.int32, (FIELDS, inner), 0)
    q1 = lax.broadcasted_iota(jnp.int32, (FIELDS, inner), 1)
    pick_q = jnp.where(q1 // ROWS == q0, 1.0, 0.0)
    spread = jnp.dot(
        jnp.dot(pick_f, coup_ref[...], precision=HIGH, preferred_element_type=jnp.float32),
        pick_q, precision=HIGH, preferred_element_type=jnp.float32,
    )
    m0 = lax.broadcasted_iota(jnp.int32, (big, inner), 0)
    m1 = lax.broadcasted_iota(jnp.int32, (big, inner), 1)
    same = (m0 // WIDE) == lax.rem(m1, ROWS)
    sea_entry = (lax.rem(m0, WIDE) == FIELDS) & (m1 // ROWS == FIELDS)
    spread = jnp.where(same, jnp.where(sea_entry, 1.0, spread), 0.0)
    spread_hi, spread_lo = halves(spread)
    spread3 = jnp.concatenate([spread_hi, spread_hi, spread_lo], axis=1)

    def second(t):
        cols = columns(t)
        get = lambda ref, side, q: [ref[side, q, :, s] for s in cols]
        state = [[get(mid, 0, c * NZ + l) for l in range(NZ)] for c in range(2)]
        others = [[mid[1, c * NZ + l, :, cols[0]] for l in range(NZ)] for c in range(2)]
        kap, wet = get(full, 0, 12), get(full, 0, 13)
        face = faces(kap, wet, full[1, 12, :, cols[0]], full[1, 13, :, cols[0]], lane, sub)
        new = mixed(state, others, face, wet[0], kv, lane, sub)
        sea = jnp.where(wet[0] > 0.0, 1.0, 0.0)
        rows = [new[c][l] * sea for c in range(2) for l in range(NZ)] + [sea]
        return new, cols[0], jnp.concatenate(rows, axis=0)

    def couple(profile):
        hi, lo = halves(profile)
        return jnp.dot(
            spread3, jnp.concatenate([hi, lo, hi], axis=0), preferred_element_type=jnp.float32
        )

    def second_loop(p, carry):
        profiles = []
        for k in range(2):
            new, here, profile = second(2 * p + k)
            profiles.append(profile)
            for c in range(2):
                for l in range(NZ):
                    next_ref[c, l, :, here] = new[c][l]
        here = pl.ds(pl.multiple_of(p * (2 * LANES), LANES), 2 * LANES)
        surf[:, here] = couple(jnp.concatenate(profiles, axis=1))
        return carry

    lax.fori_loop(0, last // 2, second_loop, 0)
    new, here, profile = second(last)
    surf[:, here] = couple(profile)
    for c in range(2):
        for l in range(NZ):
            next_ref[c, l, :, cut:length] = new[c][l][:, 0:rem]

    wlane = lax.broadcasted_iota(jnp.int32, (WIDE, LANES), 1)

    def shifted(j, cur, before):
        shift = rem * j
        if shift == 0:
            return cur
        return pltpu.roll(jnp.where(wlane < LANES - shift, cur, before), shift, 1)

    def align(t, carry):
        here = pl.ds(pl.multiple_of(t * LANES, LANES), LANES)
        prev = pl.ds(pl.multiple_of((t - 1) * LANES, LANES), LANES)
        for j in range(ROWS):
            rows = pl.ds(j * WIDE, WIDE)
            value = shifted(j, surf[rows, here], surf[rows, prev])
            blocks[last * j + t] = value.astype(jnp.bfloat16)
        return carry

    lax.fori_loop(1, last, align, 0, unroll=3)
    for j in range(ROWS + 1):
        if j > 0:
            rows = pl.ds((j - 1) * WIDE, WIDE)
            tail = shifted(j - 1, surf[rows, cut:cut + LANES], surf[rows, cut - LANES:cut])
        if j < ROWS:
            head = surf[pl.ds(j * WIDE, WIDE), 0:LANES]
            if j > 0:
                head = jnp.where(wlane >= rem * j, pltpu.roll(head, rem * j, 1), tail)
        else:
            head = tail
        blocks[last * j] = head.astype(jnp.bfloat16)

    fetch.wait()

    def product(g, carry):
        value = jnp.dot(blocks[g], weights[g], preferred_element_type=jnp.float32)
        seg = dest_ref[g] * NTILE + tile_ref[g]
        here = pl.ds(pl.multiple_of(seg * WIDE, WIDE), WIDE)
        acc[here, :] = acc[here, :] + value
        return carry

    lax.fori_loop(0, count, product, 0, unroll=25)

    owners = sums_ref.shape[0]
    quarter = owners // 4

    def deliver(d, carry):
        slot = lax.rem(d, 4)
        slot = (lax.rem(slot, 2) * 2 + slot // 2) * quarter + d // 4
        for r in range(FIELDS + 1):
            sums_ref[slot, r] = acc[pl.ds(d * (NTILE * WIDE) + r, NTILE, stride=WIDE), :]
        return carry

    lax.fori_loop(0, owners, deliver, 0)


def halo_kernel(n, *refs):
    sources, targets, (send, recv) = refs[:3], refs[3:6], refs[6:]
    me = lax.axis_index("blk")
    for target in targets:
        target[...] = jnp.zeros_like(target)

    barrier = pltpu.get_barrier_semaphore()
    sides = [(me > 0, me - 1, 0), (me < n - 1, me + 1, ROWS - 2)]
    for other in (lax.rem(me + n - 1, n), lax.rem(me + 1, n)):
        pl.semaphore_signal(
            barrier, inc=1, device_id={"blk": other}, device_id_type=pl.DeviceIdType.MESH
        )
    pl.semaphore_wait(barrier, 2)

    def copies(i):
        _, other, row = sides[i]
        found = []
        for k, (source, target) in enumerate(zip(sources, targets)):
            lead = (slice(None),) * (len(source.shape) - 2) + (pl.ds(row, 2),)
            found.append(pltpu.make_async_remote_copy(
                src_ref=source.at[lead], dst_ref=target.at[lead],
                send_sem=send.at[3 * i + k], recv_sem=recv.at[3 * i + k],
                device_id={"blk": other}, device_id_type=pl.DeviceIdType.MESH,
            ))
        return found

    for i in range(2):
        @pl.when(sides[i][0])
        def _():
            for one in copies(i):
                one.start()
    for i in range(2):
        @pl.when(sides[1 - i][0])
        def _():
            for one in copies(i):
                one.wait_recv()
    for i in range(2):
        @pl.when(sides[i][0])
        def _():
            for one in copies(i):
                one.wait_send()


def halo_part(u, kap, wet, n):
    vmem = pl.BlockSpec(memory_space=pltpu.VMEM)
    return pl.pallas_call(
        functools.partial(halo_kernel, n),
        name="halo_rows",
        out_shape=tuple(jax.ShapeDtypeStruct(x.shape, x.dtype) for x in (u, kap, wet)),
        in_specs=[pl.BlockSpec(memory_space=pl.ANY)] * 3,
        out_specs=(vmem,) * 3,
        scratch_shapes=[pltpu.SemaphoreType.DMA((6,)), pltpu.SemaphoreType.DMA((6,))],
        compiler_params=pltpu.CompilerParams(
            collective_id=1, has_side_effects=True, vmem_limit_bytes=16 * 2**20
        ),
    )(u, kap, wet)


def local_part(u, kap, wet, halo_u, halo_kap, halo_wet, kv, coup, dest, tile, weights, owners):
    length = u.shape[-1]
    pad = -(-length // LANES) * LANES
    count = weights.shape[0]
    vmem = pl.BlockSpec(memory_space=pltpu.VMEM)
    smem = pl.BlockSpec(memory_space=pltpu.SMEM)
    return pl.pallas_call(
        local_kernel,
        name="mix_and_remap",
        out_shape=(
            jax.ShapeDtypeStruct(u.shape, jnp.float32),
            jax.ShapeDtypeStruct((owners, FIELDS + 1, NTILE, AT), jnp.float32),
        ),
        in_specs=[vmem] * 6 + [smem, vmem, smem, smem, pl.BlockSpec(memory_space=pl.ANY)],
        out_specs=(vmem, vmem),
        scratch_shapes=[
            pltpu.VMEM((2, 14, ROWS, pad), jnp.float32),
            pltpu.VMEM((2, 12, ROWS, pad), jnp.float32),
            pltpu.VMEM((ROWS * WIDE, pad), jnp.float32),
            pltpu.VMEM((count, WIDE, CB), jnp.bfloat16),
            pltpu.VMEM((owners * NTILE * WIDE, AT), jnp.float32),
            pltpu.VMEM(weights.shape, jnp.bfloat16),
            pltpu.SemaphoreType.DMA,
        ],
        compiler_params=pltpu.CompilerParams(vmem_limit_bytes=44 * 2**20),
    )(u, kap, wet, halo_u, halo_kap, halo_wet, kv, coup, dest, tile, weights)


PARTS = ((0, 7), (7, 13))


def owner_kernel(n, sums_ref, out_ref, sum1, sum2, got1, got2, got3, ratio, send, recv):
    me = lax.axis_index("blk")
    quarter = n // 4
    core, side, q = lax.rem(me, 2), lax.rem(me // 2, 2), me // 4
    mate1 = me + 1 - 2 * core
    mate2 = me + 2 - 4 * side
    line = [(lax.rem(q + k, quarter)) * 4 + lax.rem(me, 4) for k in range(1, quarter)]

    barrier = pltpu.get_barrier_semaphore()
    for other in [mate1, mate2] + line:
        pl.semaphore_signal(
            barrier, inc=1, device_id={"blk": other}, device_id_type=pl.DeviceIdType.MESH
        )
    pl.semaphore_wait(barrier, 1 + quarter)

    def copy(src, dst, index, other):
        return pltpu.make_async_remote_copy(
            src_ref=src, dst_ref=dst, send_sem=send.at[index], recv_sem=recv.at[index],
            device_id={"blk": other}, device_id_type=pl.DeviceIdType.MESH,
        )

    np_ = len(PARTS)
    ones, twos, threes = [], [], []
    for i, (a, b) in enumerate(PARTS):
        rows = pl.ds(a, b - a)
        ones.append(copy(sums_ref.at[1 - core, :, :, rows], got1.at[:, :, rows], i, mate1))
        ones[-1].start()
    for i, (a, b) in enumerate(PARTS):
        rows = pl.ds(a, b - a)
        ones[i].wait_recv()
        sum1[:, :, rows] = sums_ref[core, :, :, rows] + got1[:, :, rows]
        twos.append(copy(sum1.at[1 - side, :, rows], got2.at[:, rows], np_ + i, mate2))
        twos[-1].start()
    for i, (a, b) in enumerate(PARTS):
        rows = pl.ds(a, b - a)
        twos[i].wait_recv()
        sum2[:, rows] = sum1[side, :, rows] + got2[:, rows]
        threes.append([])
        for k in range(1, quarter):
            to = lax.rem(q + k, quarter)
            threes[i].append(
                copy(sum2.at[to, rows], got3.at[k - 1, rows], 2 * np_ + (k - 1) * np_ + i, line[k - 1])
            )
            threes[i][-1].start()
    total = []
    for i, (a, b) in enumerate(PARTS):
        rows = pl.ds(a, b - a)
        value = sum2[q, rows]
        for k in range(1, quarter):
            threes[i][k - 1].wait_recv()
            value = value + got3[k - 1, rows]
        total.append(value)
    total = jnp.concatenate(total, axis=0)
    below = jnp.maximum(total[FIELDS], 1.0)
    for f in range(FIELDS):
        ratio[f * NTILE:(f + 1) * NTILE, :] = total[f] / below
    for t in range(NTILE):
        out_ref[:, t * AT:(t + 1) * AT] = ratio[pl.ds(t, FIELDS, stride=NTILE), :]
    for group in [ones, twos] + threes:
        for one in group:
            one.wait_send()


def owner_part(sums):
    n = sums.shape[0]
    quarter = n // 4
    block = sums.shape[1:]
    slots = (2 + quarter) * len(PARTS)
    vmem = pl.BlockSpec(memory_space=pltpu.VMEM)
    return pl.pallas_call(
        functools.partial(owner_kernel, n),
        name="owner_sums",
        out_shape=jax.ShapeDtypeStruct((FIELDS, NTILE * AT), jnp.float32),
        in_specs=[vmem],
        out_specs=vmem,
        scratch_shapes=[
            pltpu.VMEM((2, quarter) + block, jnp.float32),
            pltpu.VMEM((quarter,) + block, jnp.float32),
            pltpu.VMEM((2, quarter) + block, jnp.float32),
            pltpu.VMEM((quarter,) + block, jnp.float32),
            pltpu.VMEM((max(1, quarter - 1),) + block, jnp.float32),
            pltpu.VMEM((FIELDS * NTILE, AT), jnp.float32),
            pltpu.SemaphoreType.DMA((slots,)),
            pltpu.SemaphoreType.DMA((slots,)),
        ],
        compiler_params=pltpu.CompilerParams(
            collective_id=0, has_side_effects=True, vmem_limit_bytes=40 * 2**20
        ),
    )(sums.reshape((2, 2, quarter) + block))


def body(
    ocean_state, kappa_h, kappa_v, wet_depth, coupling, dest_of_block, tile_of_block, remap_weights
):
    size = lax.axis_size("blk")
    halo = halo_part(ocean_state, kappa_h, wet_depth, size)
    ocean_next, sums = local_part(
        ocean_state, kappa_h, wet_depth, *halo, kappa_v, coupling,
        dest_of_block.reshape(-1), tile_of_block, remap_weights, size,
    )
    return ocean_next, owner_part(sums)


def solution(mesh):
    return jax.shard_map(
        body,
        mesh=mesh,
        in_specs=(
            P(None, None, ("groups", "blk"), None),
            P("blk", None),
            P(),
            P("blk", None),
            P(),
            P("blk", None),
            P("blk"),
            P("blk", None, None),
        ),
        out_specs=(P(None, None, ("groups", "blk"), None), P(None, ("groups", "blk"))),
        check_vma=False,
    )
```

```python
import functools

import jax
import jax.numpy as jnp
from jax import lax
from jax.experimental import pallas as pl
from jax.experimental.pallas import tpu as pltpu
from jax.sharding import PartitionSpec as P

NZ = 6
FIELDS = 12
CB = 128
AT = 128
NTILE = 8
ROWS = 8
LANES = 128
WIDE = 16
HIGH = lax.Precision.HIGHEST


def lane_pair(cur, before, after, lane):
    east = pltpu.roll(jnp.where(lane == 0, after, cur), LANES - 1, 1)
    west = pltpu.roll(jnp.where(lane == LANES - 1, before, cur), 1, 1)
    return east, west


def row_pair(cur):
    return pltpu.roll(cur, 1, 0), pltpu.roll(cur, ROWS - 1, 0)


def faces(kap, wet, lane, sub, closed):
    nbk = lane_pair(*kap, lane) + row_pair(kap[0])
    nbw = lane_pair(*wet, lane) + row_pair(wet[0])
    depth = [jnp.minimum(wet[0], w) for w in nbw]
    if closed:
        depth[2] = jnp.where(sub == 0, 0.0, depth[2])
        depth[3] = jnp.where(sub == ROWS - 1, 0.0, depth[3])
    return [(jnp.sqrt(kap[0] * k), d) for k, d in zip(nbk, depth)]


def seam_face(kap, wet, halo_kap, halo_wet, sub):
    edge = (sub == 0) | (sub == ROWS - 1)
    root = jnp.sqrt(kap * seam(halo_kap, sub))
    return root, jnp.where(edge, jnp.minimum(wet, seam(halo_wet, sub)), 0.0)


def seam(halo, sub):
    up, down = row_pair(halo)
    return jnp.where(sub == 0, up, down)


def halves(x):
    hi = x.astype(jnp.bfloat16)
    return hi, (x - hi.astype(jnp.float32)).astype(jnp.bfloat16)


def mixed(tiles, face, wet, kv):
    out = [[None] * NZ for _ in range(2)]
    for l in range(NZ):
        coef = [jnp.where(l < depth, root, 0.0) for root, depth in face]
        below = jnp.where(l + 1 < wet, kv[l], 0.0) if l + 1 < NZ else None
        above = jnp.where(l < wet, kv[l - 1], 0.0) if l > 0 else None
        for c in range(2):
            cur = tiles[c][l][0]
            change = coef[0] * (tiles[c][l][1] - cur)
            for a, v in zip(coef[1:], tiles[c][l][2:]):
                change = change + a * (v - cur)
            if below is not None:
                change = change + below * (tiles[c][l + 1][0] - cur)
            if above is not None:
                change = change + above * (tiles[c][l - 1][0] - cur)
            out[c][l] = cur + change
    return out


def columns(t, tiles):
    def at(i):
        return pl.ds(pl.multiple_of(i * LANES, LANES), LANES)

    return [at(t), at(lax.rem(t + tiles - 1, tiles)), at(lax.rem(t + 1, tiles))]


def closed_step(src, full, dst, kv, lane, sub, tiles):
    def one(t, carry):
        cols = columns(t, tiles)
        get = lambda ref, q: [ref[0, q, :, s] for s in cols]
        state = []
        for c in range(2):
            state.append([])
            for l in range(NZ):
                cur = get(src, c * NZ + l)
                state[c].append((cur[0],) + lane_pair(*cur, lane) + row_pair(cur[0]))
        wet = get(full, 12 + 1)
        face = faces(get(full, 12), wet, lane, sub, True)
        new = mixed(state, face, wet[0], kv)
        for c in range(2):
            for l in range(NZ):
                dst[0, c * NZ + l, :, cols[0]] = new[c][l]
        return carry

    lax.fori_loop(0, tiles, one, 0)


def add_seam(value, band, halo, face, l, sub):
    coef = jnp.where(l < face[1], face[0], 0.0)
    return value + coef * (seam(halo, sub) - band)


def step_kernel(n, u_ref, kap_ref, wet_ref, kv_ref, full, mid, nxt, *refs):
    outgoing, incoming, send, recv = refs
    me = lax.axis_index("blk")
    incoming[...] = jnp.zeros_like(incoming)
    barrier = pltpu.get_barrier_semaphore()
    for other in (lax.rem(me + n - 1, n), lax.rem(me + 1, n)):
        pl.semaphore_signal(
            barrier, inc=1, device_id={"blk": other}, device_id_type=pl.DeviceIdType.MESH
        )

    length = u_ref.shape[-1]
    tiles = full.shape[-1] // LANES
    last = tiles - 1
    rem = length - last * LANES
    cut = last * LANES
    lane = lax.broadcasted_iota(jnp.int32, (ROWS, LANES), 1)
    sub = lax.broadcasted_iota(jnp.int32, (ROWS, LANES), 0)
    kv = [kv_ref[l] for l in range(NZ)]

    sides = [(me > 0, me - 1), (me < n - 1, me + 1)]

    def edge_row(far, i):
        row = (far, ROWS - 1 - far)[i]
        return slice(row, row + 1)

    def copies(far, i):
        return [pltpu.make_async_remote_copy(
            src_ref=outgoing.at[far, i], dst_ref=incoming.at[far, i],
            send_sem=send.at[far, i], recv_sem=recv.at[far, i],
            device_id={"blk": sides[i][1]}, device_id_type=pl.DeviceIdType.MESH,
        )]

    def start(far):
        for i in range(2):
            for q in range(14):
                outgoing[far, i, q:q + 1, :] = full[0, q, edge_row(far, i), :]
            @pl.when(sides[i][0])
            def _():
                for one in copies(far, i):
                    one.start()

    def arrive(far):
        for i in range(2):
            @pl.when(sides[1 - i][0])
            def _():
                for one in copies(far, i):
                    one.wait_recv()

    def spread_out(far):
        for i in range(2):
            for q in range(14):
                full[1, q, edge_row(far, i), :] = incoming[far, i, q:q + 1, :]

    def place(q, value):
        full[0, q, :, 0:cut] = value[:, 0:cut]
        tail = jnp.concatenate(
            [value[:, cut:length], jnp.zeros((ROWS, LANES - rem), jnp.float32)], axis=1
        )
        half = rem + (LANES - rem) // 2
        tail = jnp.where(
            lane < rem,
            tail,
            jnp.where(
                lane < half,
                pltpu.roll(value[:, 0:LANES], rem, 1),
                pltpu.roll(tail, LANES - rem, 1),
            ),
        )
        full[0, q, :, cut:] = tail

    for c in range(2):
        for l in range(NZ):
            place(c * NZ + l, u_ref[c, l])
    place(12, kap_ref[...])
    place(13, wet_ref[...].astype(jnp.float32))
    full[1] = jnp.zeros(full.shape[1:], jnp.float32)
    outgoing[...] = jnp.zeros_like(outgoing)
    pl.semaphore_wait(barrier, 2)
    start(0)
    closed_step(full, full, mid, kv, lane, sub, tiles)
    start(1)
    arrive(0)
    spread_out(0)

    def near(t, carry):
        here = columns(t, tiles)[0]
        face = seam_face(
            full[0, 12, :, here], full[0, 13, :, here], full[1, 12, :, here], full[1, 13, :, here], sub
        )
        for q in range(2 * NZ):
            mid[0, q, :, here] = add_seam(
                mid[0, q, :, here], full[0, q, :, here], full[1, q, :, here], face, q % NZ, sub
            )
        return carry

    lax.fori_loop(0, tiles, near, 0)
    closed_step(mid, full, nxt, kv, lane, sub, tiles)
    arrive(1)
    spread_out(1)

    def halo_step(t, carry):
        cols = columns(t, tiles)

        def get(q):
            cur = [full[1, q, :, s] for s in cols]
            band = full[0, q, :, cols[0]]
            up = pltpu.roll(jnp.where(sub == ROWS - 1, band, cur[0]), 1, 0)
            down = pltpu.roll(jnp.where(sub == 0, band, cur[0]), ROWS - 1, 0)
            return (cur[0],) + lane_pair(*cur, lane) + (up, down)

        state = [[get(c * NZ + l) for l in range(NZ)] for c in range(2)]
        kap, wet = get(12), get(13)
        face = [(jnp.sqrt(kap[0] * k), jnp.minimum(wet[0], w)) for k, w in zip(kap[1:], wet[1:])]
        new = mixed(state, face, wet[0], kv)
        for c in range(2):
            for l in range(NZ):
                mid[1, c * NZ + l, :, cols[0]] = new[c][l]
        return carry

    lax.fori_loop(0, tiles, halo_step, 0)
    for far in range(2):
        for i in range(2):
            @pl.when(sides[i][0])
            def _():
                for one in copies(far, i):
                    one.wait_send()


def step_part(u, kap, wet, kv, n):
    pad = -(-u.shape[-1] // LANES) * LANES
    vmem = pl.BlockSpec(memory_space=pltpu.VMEM)
    smem = pl.BlockSpec(memory_space=pltpu.SMEM)
    return pl.pallas_call(
        functools.partial(step_kernel, n),
        name="two_steps",
        out_shape=tuple(
            jax.ShapeDtypeStruct(x + (ROWS, pad), jnp.float32) for x in ((2, 14), (2, 12), (1, 12))
        ),
        in_specs=[vmem] * 3 + [smem],
        out_specs=(vmem,) * 3,
        scratch_shapes=[pltpu.VMEM((2, 2, 16, pad), jnp.float32)] * 2
        + [pltpu.SemaphoreType.DMA((2, 2))] * 2,
        compiler_params=pltpu.CompilerParams(
            collective_id=1, has_side_effects=True, vmem_limit_bytes=24 * 2**20
        ),
    )(u, kap, wet, kv)


def local_kernel(
    full, mid, nxt, coup_ref, dest_ref, tile_ref, w_hbm,
    next_ref, sums_ref,
    surf, blocks, acc, weights, w_sem,
):
    length = next_ref.shape[-1]
    count = w_hbm.shape[0]
    tiles = full.shape[-1] // LANES
    last = tiles - 1
    rem = length - last * LANES
    cut = last * LANES
    fetch = pltpu.make_async_copy(w_hbm, weights, w_sem)
    fetch.start()

    sub = lax.broadcasted_iota(jnp.int32, (ROWS, LANES), 0)
    acc[...] = jnp.zeros_like(acc)

    big = ROWS * WIDE
    inner = (FIELDS + 1) * ROWS
    r0 = lax.broadcasted_iota(jnp.int32, (big, FIELDS), 0)
    r1 = lax.broadcasted_iota(jnp.int32, (big, FIELDS), 1)
    pick_f = jnp.where(lax.rem(r0, WIDE) == r1, 1.0, 0.0)
    q0 = lax.broadcasted_iota(jnp.int32, (FIELDS, inner), 0)
    q1 = lax.broadcasted_iota(jnp.int32, (FIELDS, inner), 1)
    pick_q = jnp.where(q1 // ROWS == q0, 1.0, 0.0)
    spread = jnp.dot(
        jnp.dot(pick_f, coup_ref[...], precision=HIGH, preferred_element_type=jnp.float32),
        pick_q, precision=HIGH, preferred_element_type=jnp.float32,
    )
    m0 = lax.broadcasted_iota(jnp.int32, (big, inner), 0)
    m1 = lax.broadcasted_iota(jnp.int32, (big, inner), 1)
    same = (m0 // WIDE) == lax.rem(m1, ROWS)
    sea_entry = (lax.rem(m0, WIDE) == FIELDS) & (m1 // ROWS == FIELDS)
    spread = jnp.where(same, jnp.where(sea_entry, 1.0, spread), 0.0)
    spread_hi, spread_lo = halves(spread)
    spread3 = jnp.concatenate([spread_hi, spread_hi, spread_lo], axis=1)

    def second(t):
        here = columns(t, tiles)[0]
        wet = full[0, 13, :, here]
        face = seam_face(full[0, 12, :, here], wet, full[1, 12, :, here], full[1, 13, :, here], sub)
        new = [
            add_seam(nxt[0, q, :, here], mid[0, q, :, here], mid[1, q, :, here], face, q % NZ, sub)
            for q in range(2 * NZ)
        ]
        new = [new[:NZ], new[NZ:]]
        sea = jnp.where(wet > 0.0, 1.0, 0.0)
        rows = [new[c][l] * sea for c in range(2) for l in range(NZ)] + [sea]
        return new, here, jnp.concatenate(rows, axis=0)

    def couple(profile):
        hi, lo = halves(profile)
        return jnp.dot(
            spread3, jnp.concatenate([hi, lo, hi], axis=0), preferred_element_type=jnp.float32
        )

    def second_loop(p, carry):
        profiles = []
        for k in range(2):
            new, here, profile = second(2 * p + k)
            profiles.append(profile)
            for c in range(2):
                for l in range(NZ):
                    next_ref[c, l, :, here] = new[c][l]
        here = pl.ds(pl.multiple_of(p * (2 * LANES), LANES), 2 * LANES)
        surf[:, here] = couple(jnp.concatenate(profiles, axis=1))
        return carry

    lax.fori_loop(0, last // 2, second_loop, 0)
    new, here, profile = second(last)
    surf[:, here] = couple(profile)
    for c in range(2):
        for l in range(NZ):
            next_ref[c, l, :, cut:length] = new[c][l][:, 0:rem]

    wlane = lax.broadcasted_iota(jnp.int32, (WIDE, LANES), 1)

    def shifted(j, cur, before):
        shift = rem * j
        if shift == 0:
            return cur
        return pltpu.roll(jnp.where(wlane < LANES - shift, cur, before), shift, 1)

    def align(t, carry):
        here = pl.ds(pl.multiple_of(t * LANES, LANES), LANES)
        prev = pl.ds(pl.multiple_of((t - 1) * LANES, LANES), LANES)
        for j in range(ROWS):
            rows = pl.ds(j * WIDE, WIDE)
            value = shifted(j, surf[rows, here], surf[rows, prev])
            blocks[last * j + t] = value.astype(jnp.bfloat16)
        return carry

    lax.fori_loop(1, last, align, 0, unroll=3)
    for j in range(ROWS + 1):
        if j > 0:
            rows = pl.ds((j - 1) * WIDE, WIDE)
            tail = shifted(j - 1, surf[rows, cut:cut + LANES], surf[rows, cut - LANES:cut])
        if j < ROWS:
            head = surf[pl.ds(j * WIDE, WIDE), 0:LANES]
            if j > 0:
                head = jnp.where(wlane >= rem * j, pltpu.roll(head, rem * j, 1), tail)
        else:
            head = tail
        blocks[last * j] = head.astype(jnp.bfloat16)

    fetch.wait()

    def product(g, carry):
        value = jnp.dot(blocks[g], weights[g], preferred_element_type=jnp.float32)
        seg = dest_ref[g] * NTILE + tile_ref[g]
        here = pl.ds(pl.multiple_of(seg * WIDE, WIDE), WIDE)
        acc[here, :] = acc[here, :] + value
        return carry

    lax.fori_loop(0, count, product, 0, unroll=25)

    owners = sums_ref.shape[0]
    quarter = owners // 4

    def deliver(d, carry):
        slot = lax.rem(d, 4)
        slot = (lax.rem(slot, 2) * 2 + slot // 2) * quarter + d // 4
        for r in range(FIELDS + 1):
            sums_ref[slot, r] = acc[pl.ds(d * (NTILE * WIDE) + r, NTILE, stride=WIDE), :]
        return carry

    lax.fori_loop(0, owners, deliver, 0)


def local_part(full, mid, nxt, coup, dest, tile, weights, length, owners):
    pad = full.shape[-1]
    count = weights.shape[0]
    vmem = pl.BlockSpec(memory_space=pltpu.VMEM)
    smem = pl.BlockSpec(memory_space=pltpu.SMEM)
    return pl.pallas_call(
        local_kernel,
        name="remap",
        out_shape=(
            jax.ShapeDtypeStruct((2, NZ, ROWS, length), jnp.float32),
            jax.ShapeDtypeStruct((owners, FIELDS + 1, NTILE, AT), jnp.float32),
        ),
        in_specs=[vmem] * 4 + [smem, smem, pl.BlockSpec(memory_space=pl.ANY)],
        out_specs=(vmem, vmem),
        scratch_shapes=[
            pltpu.VMEM((ROWS * WIDE, pad), jnp.float32),
            pltpu.VMEM((count, WIDE, CB), jnp.bfloat16),
            pltpu.VMEM((owners * NTILE * WIDE, AT), jnp.float32),
            pltpu.VMEM(weights.shape, jnp.bfloat16),
            pltpu.SemaphoreType.DMA,
        ],
        compiler_params=pltpu.CompilerParams(vmem_limit_bytes=44 * 2**20),
    )(full, mid, nxt, coup, dest, tile, weights)


PARTS = ((0, 4), (4, 7), (7, 10), (10, 13))


def owner_kernel(n, sums_ref, out_ref, sum1, sum2, got1, got2, got3, ratio, send, recv):
    me = lax.axis_index("blk")
    quarter = n // 4
    core, side, q = lax.rem(me, 2), lax.rem(me // 2, 2), me // 4
    mate1 = me + 1 - 2 * core
    mate2 = me + 2 - 4 * side
    line = [(lax.rem(q + k, quarter)) * 4 + lax.rem(me, 4) for k in range(1, quarter)]

    barrier = pltpu.get_barrier_semaphore()
    for other in [mate1, mate2] + line:
        pl.semaphore_signal(
            barrier, inc=1, device_id={"blk": other}, device_id_type=pl.DeviceIdType.MESH
        )
    pl.semaphore_wait(barrier, 1 + quarter)

    def copy(src, dst, index, other):
        return pltpu.make_async_remote_copy(
            src_ref=src, dst_ref=dst, send_sem=send.at[index], recv_sem=recv.at[index],
            device_id={"blk": other}, device_id_type=pl.DeviceIdType.MESH,
        )

    np_ = len(PARTS)
    ones, twos, threes = [], [], []
    for i, (a, b) in enumerate(PARTS):
        rows = pl.ds(a, b - a)
        ones.append(copy(sums_ref.at[1 - core, :, :, rows], got1.at[:, :, rows], i, mate1))
        ones[-1].start()
    for i, (a, b) in enumerate(PARTS):
        rows = pl.ds(a, b - a)
        ones[i].wait_recv()
        sum1[:, :, rows] = sums_ref[core, :, :, rows] + got1[:, :, rows]
        twos.append(copy(sum1.at[1 - side, :, rows], got2.at[:, rows], np_ + i, mate2))
        twos[-1].start()
    for i, (a, b) in enumerate(PARTS):
        rows = pl.ds(a, b - a)
        twos[i].wait_recv()
        sum2[:, rows] = sum1[side, :, rows] + got2[:, rows]
        threes.append([])
        for k in range(1, quarter):
            to = lax.rem(q + k, quarter)
            threes[i].append(
                copy(sum2.at[to, rows], got3.at[k - 1, rows], 2 * np_ + (k - 1) * np_ + i, line[k - 1])
            )
            threes[i][-1].start()
    total = []
    for i, (a, b) in enumerate(PARTS):
        rows = pl.ds(a, b - a)
        value = sum2[q, rows]
        for k in range(1, quarter):
            threes[i][k - 1].wait_recv()
            value = value + got3[k - 1, rows]
        total.append(value)
    total = jnp.concatenate(total, axis=0)
    below = jnp.maximum(total[FIELDS], 1.0)
    for f in range(FIELDS):
        ratio[f * NTILE:(f + 1) * NTILE, :] = total[f] / below
    for t in range(NTILE):
        out_ref[:, t * AT:(t + 1) * AT] = ratio[pl.ds(t, FIELDS, stride=NTILE), :]
    for group in [ones, twos] + threes:
        for one in group:
            one.wait_send()


def owner_part(sums):
    n = sums.shape[0]
    quarter = n // 4
    block = sums.shape[1:]
    slots = (2 + quarter) * len(PARTS)
    vmem = pl.BlockSpec(memory_space=pltpu.VMEM)
    return pl.pallas_call(
        functools.partial(owner_kernel, n),
        name="owner_sums",
        out_shape=jax.ShapeDtypeStruct((FIELDS, NTILE * AT), jnp.float32),
        in_specs=[vmem],
        out_specs=vmem,
        scratch_shapes=[
            pltpu.VMEM((2, quarter) + block, jnp.float32),
            pltpu.VMEM((quarter,) + block, jnp.float32),
            pltpu.VMEM((2, quarter) + block, jnp.float32),
            pltpu.VMEM((quarter,) + block, jnp.float32),
            pltpu.VMEM((max(1, quarter - 1),) + block, jnp.float32),
            pltpu.VMEM((FIELDS * NTILE, AT), jnp.float32),
            pltpu.SemaphoreType.DMA((slots,)),
            pltpu.SemaphoreType.DMA((slots,)),
        ],
        compiler_params=pltpu.CompilerParams(
            collective_id=0, has_side_effects=True, vmem_limit_bytes=40 * 2**20
        ),
    )(sums.reshape((2, 2, quarter) + block))


def body(
    ocean_state, kappa_h, kappa_v, wet_depth, coupling, dest_of_block, tile_of_block, remap_weights
):
    size = lax.axis_size("blk")
    steps = step_part(ocean_state, kappa_h, wet_depth, kappa_v, size)
    ocean_next, sums = local_part(
        *steps, coupling, dest_of_block.reshape(-1), tile_of_block, remap_weights,
        ocean_state.shape[-1], size,
    )
    return ocean_next, owner_part(sums)


def solution(mesh):
    return jax.shard_map(
        body,
        mesh=mesh,
        in_specs=(
            P(None, None, ("groups", "blk"), None),
            P("blk", None),
            P(),
            P("blk", None),
            P(),
            P("blk", None),
            P("blk"),
            P("blk", None, None),
        ),
        out_specs=(P(None, None, ("groups", "blk"), None), P(None, ("groups", "blk"))),
        check_vma=False,
    )
```

```python
import functools

import jax
import jax.numpy as jnp
from jax import lax
from jax.experimental import pallas as pl
from jax.experimental.pallas import tpu as pltpu
from jax.sharding import PartitionSpec as P

NZ = 6
FIELDS = 12
CB = 128
AT = 128
NTILE = 8
ROWS = 8
LANES = 128
WIDE = 16
HIGH = lax.Precision.HIGHEST


def lane_pair(cur, before, after, lane):
    east = pltpu.roll(jnp.where(lane == 0, after, cur), LANES - 1, 1)
    west = pltpu.roll(jnp.where(lane == LANES - 1, before, cur), 1, 1)
    return east, west


def row_pair(cur):
    return pltpu.roll(cur, 1, 0), pltpu.roll(cur, ROWS - 1, 0)


def faces(kap, wet, lane, sub, closed):
    nbk = lane_pair(*kap, lane) + row_pair(kap[0])
    nbw = lane_pair(*wet, lane) + row_pair(wet[0])
    depth = [jnp.minimum(wet[0], w) for w in nbw]
    if closed:
        depth[2] = jnp.where(sub == 0, 0.0, depth[2])
        depth[3] = jnp.where(sub == ROWS - 1, 0.0, depth[3])
    return [(jnp.sqrt(kap[0] * k), d) for k, d in zip(nbk, depth)]


def seam_face(kap, wet, halo_kap, halo_wet, sub):
    edge = (sub == 0) | (sub == ROWS - 1)
    root = jnp.sqrt(kap * seam(halo_kap, sub))
    return root, jnp.where(edge, jnp.minimum(wet, seam(halo_wet, sub)), 0.0)


def seam(halo, sub):
    up, down = row_pair(halo)
    return jnp.where(sub == 0, up, down)


def halves(x):
    hi = x.astype(jnp.bfloat16)
    return hi, (x - hi.astype(jnp.float32)).astype(jnp.bfloat16)


def mixed(tiles, face, wet, kv):
    out = [[None] * NZ for _ in range(2)]
    for l in range(NZ):
        coef = [jnp.where(l < depth, root, 0.0) for root, depth in face]
        below = jnp.where(l + 1 < wet, kv[l], 0.0) if l + 1 < NZ else None
        above = jnp.where(l < wet, kv[l - 1], 0.0) if l > 0 else None
        for c in range(2):
            cur = tiles[c][l][0]
            change = coef[0] * (tiles[c][l][1] - cur)
            for a, v in zip(coef[1:], tiles[c][l][2:]):
                change = change + a * (v - cur)
            if below is not None:
                change = change + below * (tiles[c][l + 1][0] - cur)
            if above is not None:
                change = change + above * (tiles[c][l - 1][0] - cur)
            out[c][l] = cur + change
    return out


def columns(t, tiles):
    def at(i):
        return pl.ds(pl.multiple_of(i * LANES, LANES), LANES)

    return [at(t), at(lax.rem(t + tiles - 1, tiles)), at(lax.rem(t + 1, tiles))]


def closed_step(src, full, dst, kv, lane, sub, tiles):
    def one(t, carry):
        cols = columns(t, tiles)
        get = lambda ref, q: [ref[0, q, :, s] for s in cols]
        state = []
        for c in range(2):
            state.append([])
            for l in range(NZ):
                cur = get(src, c * NZ + l)
                state[c].append((cur[0],) + lane_pair(*cur, lane) + row_pair(cur[0]))
        wet = get(full, 12 + 1)
        face = faces(get(full, 12), wet, lane, sub, True)
        new = mixed(state, face, wet[0], kv)
        for c in range(2):
            for l in range(NZ):
                dst[0, c * NZ + l, :, cols[0]] = new[c][l]
        return carry

    lax.fori_loop(0, tiles, one, 0)


def seam_coef(face, l):
    return jnp.where(l < face[1], face[0], 0.0)


def step_kernel(n, u_ref, kap_ref, wet_ref, kv_ref, full, mid, nxt, *refs):
    outgoing, incoming, send, recv = refs
    me = lax.axis_index("blk")
    incoming[...] = jnp.zeros_like(incoming)
    barrier = pltpu.get_barrier_semaphore()
    for other in (lax.rem(me + n - 1, n), lax.rem(me + 1, n)):
        pl.semaphore_signal(
            barrier, inc=1, device_id={"blk": other}, device_id_type=pl.DeviceIdType.MESH
        )

    length = u_ref.shape[-1]
    tiles = full.shape[-1] // LANES
    last = tiles - 1
    rem = length - last * LANES
    cut = last * LANES
    lane = lax.broadcasted_iota(jnp.int32, (ROWS, LANES), 1)
    sub = lax.broadcasted_iota(jnp.int32, (ROWS, LANES), 0)
    kv = [kv_ref[l] for l in range(NZ)]

    sides = [(me > 0, me - 1), (me < n - 1, me + 1)]

    def edge_row(i):
        row = (0, ROWS - 1)[i]
        return slice(row, row + 1)

    def copies(far, i):
        return [pltpu.make_async_remote_copy(
            src_ref=outgoing.at[far, i], dst_ref=incoming.at[far, i],
            send_sem=send.at[far, i], recv_sem=recv.at[far, i],
            device_id={"blk": sides[i][1]}, device_id_type=pl.DeviceIdType.MESH,
        )]

    def start(far, source, rows):
        for i in range(2):
            for q in range(rows):
                outgoing[far, i, q:q + 1, :] = source[0, q, edge_row(i), :]

            @pl.when(sides[i][0])
            def _():
                for one in copies(far, i):
                    one.start()

    def arrive(far):
        for i in range(2):
            @pl.when(sides[1 - i][0])
            def _():
                for one in copies(far, i):
                    one.wait_recv()

    def spread_out(far, target, rows):
        for i in range(2):
            for q in range(rows):
                target[1, q, edge_row(i), :] = incoming[far, i, q:q + 1, :]

    def place(q, value):
        full[0, q, :, 0:cut] = value[:, 0:cut]
        tail = jnp.concatenate(
            [value[:, cut:length], jnp.zeros((ROWS, LANES - rem), jnp.float32)], axis=1
        )
        half = rem + (LANES - rem) // 2
        tail = jnp.where(
            lane < rem,
            tail,
            jnp.where(
                lane < half,
                pltpu.roll(value[:, 0:LANES], rem, 1),
                pltpu.roll(tail, LANES - rem, 1),
            ),
        )
        full[0, q, :, cut:] = tail

    for c in range(2):
        for l in range(NZ):
            place(c * NZ + l, u_ref[c, l])
    place(12, kap_ref[...])
    place(13, wet_ref[...].astype(jnp.float32))
    full[1] = jnp.zeros(full.shape[1:], jnp.float32)
    outgoing[...] = jnp.zeros_like(outgoing)
    pl.semaphore_wait(barrier, 2)
    start(0, full, 14)
    closed_step(full, full, mid, kv, lane, sub, tiles)
    start(1, mid, 2 * NZ)
    mid[1] = jnp.zeros(mid.shape[1:], jnp.float32)
    arrive(0)
    spread_out(0, full, 14)

    def near(t, carry):
        here = columns(t, tiles)[0]
        face = seam_face(
            full[0, 12, :, here], full[0, 13, :, here], full[1, 12, :, here], full[1, 13, :, here], sub
        )
        for q in range(2 * NZ):
            flux = seam_coef(face, q % NZ) * (seam(full[1, q, :, here], sub) - full[0, q, :, here])
            mid[0, q, :, here] = mid[0, q, :, here] + flux
        return carry

    lax.fori_loop(0, tiles, near, 0)
    closed_step(mid, full, nxt, kv, lane, sub, tiles)
    arrive(1)
    spread_out(1, mid, 2 * NZ)
    for far in range(2):
        for i in range(2):
            @pl.when(sides[i][0])
            def _():
                for one in copies(far, i):
                    one.wait_send()


def step_part(u, kap, wet, kv, n):
    pad = -(-u.shape[-1] // LANES) * LANES
    vmem = pl.BlockSpec(memory_space=pltpu.VMEM)
    smem = pl.BlockSpec(memory_space=pltpu.SMEM)
    return pl.pallas_call(
        functools.partial(step_kernel, n),
        name="two_steps",
        cost_estimate=pl.CostEstimate(flops=20000000, bytes_accessed=12000000, transcendentals=0),
        out_shape=tuple(
            jax.ShapeDtypeStruct(x + (ROWS, pad), jnp.float32) for x in ((2, 14), (2, 12), (1, 12))
        ),
        in_specs=[vmem] * 3 + [smem],
        out_specs=(vmem,) * 3,
        scratch_shapes=[pltpu.VMEM((2, 2, 16, pad), jnp.float32)] * 2
        + [pltpu.SemaphoreType.DMA((2, 2))] * 2,
        compiler_params=pltpu.CompilerParams(
            collective_id=1, has_side_effects=True, vmem_limit_bytes=24 * 2**20
        ),
    )(u, kap, wet, kv)


def local_kernel(
    full, mid, nxt, coup_ref, dest_ref, tile_ref, w_hbm,
    next_ref, sums_ref,
    surf, blocks, acc, weights, w_sem,
):
    length = next_ref.shape[-1]
    count = w_hbm.shape[0]
    tiles = full.shape[-1] // LANES
    last = tiles - 1
    rem = length - last * LANES
    cut = last * LANES
    fetch = pltpu.make_async_copy(w_hbm, weights, w_sem)
    fetch.start()

    sub = lax.broadcasted_iota(jnp.int32, (ROWS, LANES), 0)
    acc[...] = jnp.zeros_like(acc)

    big = ROWS * WIDE
    inner = (FIELDS + 1) * ROWS
    r0 = lax.broadcasted_iota(jnp.int32, (big, FIELDS), 0)
    r1 = lax.broadcasted_iota(jnp.int32, (big, FIELDS), 1)
    pick_f = jnp.where(lax.rem(r0, WIDE) == r1, 1.0, 0.0)
    q0 = lax.broadcasted_iota(jnp.int32, (FIELDS, inner), 0)
    q1 = lax.broadcasted_iota(jnp.int32, (FIELDS, inner), 1)
    pick_q = jnp.where(q1 // ROWS == q0, 1.0, 0.0)
    spread = jnp.dot(
        jnp.dot(pick_f, coup_ref[...], precision=HIGH, preferred_element_type=jnp.float32),
        pick_q, precision=HIGH, preferred_element_type=jnp.float32,
    )
    m0 = lax.broadcasted_iota(jnp.int32, (big, inner), 0)
    m1 = lax.broadcasted_iota(jnp.int32, (big, inner), 1)
    same = (m0 // WIDE) == lax.rem(m1, ROWS)
    sea_entry = (lax.rem(m0, WIDE) == FIELDS) & (m1 // ROWS == FIELDS)
    spread = jnp.where(same, jnp.where(sea_entry, 1.0, spread), 0.0)
    spread_hi, spread_lo = halves(spread)
    spread3 = jnp.concatenate([spread_hi, spread_hi, spread_lo], axis=1)

    def second(t):
        here = columns(t, tiles)[0]
        wet = full[0, 13, :, here]
        face = seam_face(full[0, 12, :, here], wet, full[1, 12, :, here], full[1, 13, :, here], sub)
        new = []
        for q in range(2 * NZ):
            coef = seam_coef(face, q % NZ)
            flux = coef * (seam(full[1, q, :, here], sub) - full[0, q, :, here])
            beyond = seam(mid[1, q, :, here], sub) - flux
            new.append(nxt[0, q, :, here] + coef * (beyond - mid[0, q, :, here]))
        new = [new[:NZ], new[NZ:]]
        sea = jnp.where(wet > 0.0, 1.0, 0.0)
        rows = [new[c][l] * sea for c in range(2) for l in range(NZ)] + [sea]
        return new, here, jnp.concatenate(rows, axis=0)

    def couple(profile):
        hi, lo = halves(profile)
        return jnp.dot(
            spread3, jnp.concatenate([hi, lo, hi], axis=0), preferred_element_type=jnp.float32
        )

    def second_loop(p, carry):
        profiles = []
        for k in range(2):
            new, here, profile = second(2 * p + k)
            profiles.append(profile)
            for c in range(2):
                for l in range(NZ):
                    next_ref[c, l, :, here] = new[c][l]
        here = pl.ds(pl.multiple_of(p * (2 * LANES), LANES), 2 * LANES)
        surf[:, here] = couple(jnp.concatenate(profiles, axis=1))
        return carry

    lax.fori_loop(0, last // 2, second_loop, 0)
    new, here, profile = second(last)
    surf[:, here] = couple(profile)
    for c in range(2):
        for l in range(NZ):
            next_ref[c, l, :, cut:length] = new[c][l][:, 0:rem]

    wlane = lax.broadcasted_iota(jnp.int32, (WIDE, LANES), 1)

    def shifted(j, cur, before):
        shift = rem * j
        if shift == 0:
            return cur
        return pltpu.roll(jnp.where(wlane < LANES - shift, cur, before), shift, 1)

    def align(t, carry):
        here = pl.ds(pl.multiple_of(t * LANES, LANES), LANES)
        prev = pl.ds(pl.multiple_of((t - 1) * LANES, LANES), LANES)
        for j in range(ROWS):
            rows = pl.ds(j * WIDE, WIDE)
            value = shifted(j, surf[rows, here], surf[rows, prev])
            blocks[last * j + t] = value.astype(jnp.bfloat16)
        return carry

    lax.fori_loop(1, last, align, 0, unroll=3)
    for j in range(ROWS + 1):
        if j > 0:
            rows = pl.ds((j - 1) * WIDE, WIDE)
            tail = shifted(j - 1, surf[rows, cut:cut + LANES], surf[rows, cut - LANES:cut])
        if j < ROWS:
            head = surf[pl.ds(j * WIDE, WIDE), 0:LANES]
            if j > 0:
                head = jnp.where(wlane >= rem * j, pltpu.roll(head, rem * j, 1), tail)
        else:
            head = tail
        blocks[last * j] = head.astype(jnp.bfloat16)

    fetch.wait()

    def product(g, carry):
        value = jnp.dot(blocks[g], weights[g], preferred_element_type=jnp.float32)
        seg = dest_ref[g] * NTILE + tile_ref[g]
        here = pl.ds(pl.multiple_of(seg * WIDE, WIDE), WIDE)
        acc[here, :] = acc[here, :] + value
        return carry

    lax.fori_loop(0, count, product, 0, unroll=25)

    owners = sums_ref.shape[0]
    quarter = owners // 4

    def deliver(d, carry):
        slot = lax.rem(d, 4)
        slot = (lax.rem(slot, 2) * 2 + slot // 2) * quarter + d // 4
        for r in range(FIELDS + 1):
            sums_ref[slot, r] = acc[pl.ds(d * (NTILE * WIDE) + r, NTILE, stride=WIDE), :]
        return carry

    lax.fori_loop(0, owners, deliver, 0)


def local_part(full, mid, nxt, coup, dest, tile, weights, length, owners):
    pad = full.shape[-1]
    count = weights.shape[0]
    vmem = pl.BlockSpec(memory_space=pltpu.VMEM)
    smem = pl.BlockSpec(memory_space=pltpu.SMEM)
    return pl.pallas_call(
        local_kernel,
        name="remap",
        cost_estimate=pl.CostEstimate(flops=200000000, bytes_accessed=18000000, transcendentals=0),
        out_shape=(
            jax.ShapeDtypeStruct((2, NZ, ROWS, length), jnp.float32),
            jax.ShapeDtypeStruct((owners, FIELDS + 1, NTILE, AT), jnp.float32),
        ),
        in_specs=[vmem] * 4 + [smem, smem, pl.BlockSpec(memory_space=pl.ANY)],
        out_specs=(vmem, vmem),
        scratch_shapes=[
            pltpu.VMEM((ROWS * WIDE, pad), jnp.float32),
            pltpu.VMEM((count, WIDE, CB), jnp.bfloat16),
            pltpu.VMEM((owners * NTILE * WIDE, AT), jnp.float32),
            pltpu.VMEM(weights.shape, jnp.bfloat16),
            pltpu.SemaphoreType.DMA,
        ],
        compiler_params=pltpu.CompilerParams(vmem_limit_bytes=44 * 2**20),
    )(full, mid, nxt, coup, dest, tile, weights)


PARTS = ((0, 4), (4, 7), (7, 10), (10, 13))


def owner_kernel(n, sums_ref, out_ref, sum1, sum2, got1, got2, got3, ratio, send, recv):
    me = lax.axis_index("blk")
    quarter = n // 4
    core, side, q = lax.rem(me, 2), lax.rem(me // 2, 2), me // 4
    mate1 = me + 1 - 2 * core
    mate2 = me + 2 - 4 * side
    line = [(lax.rem(q + k, quarter)) * 4 + lax.rem(me, 4) for k in range(1, quarter)]

    barrier = pltpu.get_barrier_semaphore()
    for other in [mate1, mate2] + line:
        pl.semaphore_signal(
            barrier, inc=1, device_id={"blk": other}, device_id_type=pl.DeviceIdType.MESH
        )
    pl.semaphore_wait(barrier, 1 + quarter)

    def copy(src, dst, index, other):
        return pltpu.make_async_remote_copy(
            src_ref=src, dst_ref=dst, send_sem=send.at[index], recv_sem=recv.at[index],
            device_id={"blk": other}, device_id_type=pl.DeviceIdType.MESH,
        )

    np_ = len(PARTS)
    ones, twos, threes = [], [], []
    for i, (a, b) in enumerate(PARTS):
        rows = pl.ds(a, b - a)
        ones.append(copy(sums_ref.at[1 - core, :, :, rows], got1.at[:, :, rows], i, mate1))
        ones[-1].start()
    for i, (a, b) in enumerate(PARTS):
        rows = pl.ds(a, b - a)
        ones[i].wait_recv()
        sum1[:, :, rows] = sums_ref[core, :, :, rows] + got1[:, :, rows]
        twos.append(copy(sum1.at[1 - side, :, rows], got2.at[:, rows], np_ + i, mate2))
        twos[-1].start()
    for i, (a, b) in enumerate(PARTS):
        rows = pl.ds(a, b - a)
        twos[i].wait_recv()
        sum2[:, rows] = sum1[side, :, rows] + got2[:, rows]
        threes.append([])
        for k in range(1, quarter):
            to = lax.rem(q + k, quarter)
            threes[i].append(
                copy(sum2.at[to, rows], got3.at[k - 1, rows], 2 * np_ + (k - 1) * np_ + i, line[k - 1])
            )
            threes[i][-1].start()
    total = []
    for i, (a, b) in enumerate(PARTS):
        rows = pl.ds(a, b - a)
        value = sum2[q, rows]
        for k in range(1, quarter):
            threes[i][k - 1].wait_recv()
            value = value + got3[k - 1, rows]
        total.append(value)
    total = jnp.concatenate(total, axis=0)
    below = jnp.maximum(total[FIELDS], 1.0)
    for f in range(FIELDS):
        ratio[f * NTILE:(f + 1) * NTILE, :] = total[f] / below
    for t in range(NTILE):
        out_ref[:, t * AT:(t + 1) * AT] = ratio[pl.ds(t, FIELDS, stride=NTILE), :]
    for group in [ones, twos] + threes:
        for one in group:
            one.wait_send()


def owner_part(sums):
    n = sums.shape[0]
    quarter = n // 4
    block = sums.shape[1:]
    slots = (2 + quarter) * len(PARTS)
    vmem = pl.BlockSpec(memory_space=pltpu.VMEM)
    return pl.pallas_call(
        functools.partial(owner_kernel, n),
        name="owner_sums",
        cost_estimate=pl.CostEstimate(flops=1000000, bytes_accessed=4000000, transcendentals=0),
        out_shape=jax.ShapeDtypeStruct((FIELDS, NTILE * AT), jnp.float32),
        in_specs=[vmem],
        out_specs=vmem,
        scratch_shapes=[
            pltpu.VMEM((2, quarter) + block, jnp.float32),
            pltpu.VMEM((quarter,) + block, jnp.float32),
            pltpu.VMEM((2, quarter) + block, jnp.float32),
            pltpu.VMEM((quarter,) + block, jnp.float32),
            pltpu.VMEM((max(1, quarter - 1),) + block, jnp.float32),
            pltpu.VMEM((FIELDS * NTILE, AT), jnp.float32),
            pltpu.SemaphoreType.DMA((slots,)),
            pltpu.SemaphoreType.DMA((slots,)),
        ],
        compiler_params=pltpu.CompilerParams(
            collective_id=0, has_side_effects=True, vmem_limit_bytes=40 * 2**20
        ),
    )(sums.reshape((2, 2, quarter) + block))


def body(
    ocean_state, kappa_h, kappa_v, wet_depth, coupling, dest_of_block, tile_of_block, remap_weights
):
    size = lax.axis_size("blk")
    steps = step_part(ocean_state, kappa_h, wet_depth, kappa_v, size)
    ocean_next, sums = local_part(
        *steps, coupling, dest_of_block.reshape(-1), tile_of_block, remap_weights,
        ocean_state.shape[-1], size,
    )
    return ocean_next, owner_part(sums)


def solution(mesh):
    return jax.shard_map(
        body,
        mesh=mesh,
        in_specs=(
            P(None, None, ("groups", "blk"), None),
            P("blk", None),
            P(),
            P("blk", None),
            P(),
            P("blk", None),
            P("blk"),
            P("blk", None, None),
        ),
        out_specs=(P(None, None, ("groups", "blk"), None), P(None, ("groups", "blk"))),
        check_vma=False,
    )
```

```python
import functools

import jax
import jax.numpy as jnp
from jax import lax
from jax.experimental import pallas as pl
from jax.experimental.pallas import tpu as pltpu
from jax.sharding import PartitionSpec as P

NZ = 6
FIELDS = 12
CB = 128
AT = 128
NTILE = 8
ROWS = 8
LANES = 128
WIDE = 16
HIGH = lax.Precision.HIGHEST


def lane_pair(cur, before, after, lane):
    east = pltpu.roll(jnp.where(lane == 0, after, cur), LANES - 1, 1)
    west = pltpu.roll(jnp.where(lane == LANES - 1, before, cur), 1, 1)
    return east, west


def row_pair(cur):
    return pltpu.roll(cur, 1, 0), pltpu.roll(cur, ROWS - 1, 0)


def faces(kap, wet, lane, sub, closed):
    nbk = lane_pair(*kap, lane) + row_pair(kap[0])
    nbw = lane_pair(*wet, lane) + row_pair(wet[0])
    depth = [jnp.minimum(wet[0], w) for w in nbw]
    if closed:
        depth[2] = jnp.where(sub == 0, 0.0, depth[2])
        depth[3] = jnp.where(sub == ROWS - 1, 0.0, depth[3])
    return [(jnp.sqrt(kap[0] * k), d) for k, d in zip(nbk, depth)]


def seam_face(kap, wet, halo_kap, halo_wet, sub):
    edge = (sub == 0) | (sub == ROWS - 1)
    root = jnp.sqrt(kap * seam(halo_kap, sub))
    return root, jnp.where(edge, jnp.minimum(wet, seam(halo_wet, sub)), 0.0)


def seam(halo, sub):
    up, down = row_pair(halo)
    return jnp.where(sub == 0, up, down)


def halves(x):
    hi = x.astype(jnp.bfloat16)
    return hi, (x - hi.astype(jnp.float32)).astype(jnp.bfloat16)


def mixed(tiles, face, wet, kv):
    out = [[None] * NZ for _ in range(2)]
    for l in range(NZ):
        coef = [jnp.where(l < depth, root, 0.0) for root, depth in face]
        below = jnp.where(l + 1 < wet, kv[l], 0.0) if l + 1 < NZ else None
        above = jnp.where(l < wet, kv[l - 1], 0.0) if l > 0 else None
        for c in range(2):
            cur = tiles[c][l][0]
            change = coef[0] * (tiles[c][l][1] - cur)
            for a, v in zip(coef[1:], tiles[c][l][2:]):
                change = change + a * (v - cur)
            if below is not None:
                change = change + below * (tiles[c][l + 1][0] - cur)
            if above is not None:
                change = change + above * (tiles[c][l - 1][0] - cur)
            out[c][l] = cur + change
    return out


def columns(t, tiles):
    def at(i):
        return pl.ds(pl.multiple_of(i * LANES, LANES), LANES)

    return [at(t), at(lax.rem(t + tiles - 1, tiles)), at(lax.rem(t + 1, tiles))]


def closed_step(src, full, dst, kv, lane, sub, tiles):
    def one(t, carry):
        cols = columns(t, tiles)
        get = lambda ref, q: [ref[0, q, :, s] for s in cols]
        state = []
        for c in range(2):
            state.append([])
            for l in range(NZ):
                cur = get(src, c * NZ + l)
                state[c].append((cur[0],) + lane_pair(*cur, lane) + row_pair(cur[0]))
        wet = get(full, 12 + 1)
        face = faces(get(full, 12), wet, lane, sub, True)
        new = mixed(state, face, wet[0], kv)
        for c in range(2):
            for l in range(NZ):
                dst[0, c * NZ + l, :, cols[0]] = new[c][l]
        return carry

    lax.fori_loop(0, tiles, one, 0)


def seam_coef(face, l):
    return jnp.where(l < face[1], face[0], 0.0)


GROUPS = (((0, 8), (8, 4), (12, 2)), ((0, 8), (8, 4)))
N_GROUPS = sum(len(groups) for groups in GROUPS)


def step_kernel(n, u_ref, kap_ref, wet_ref, kv_ref, full, mid, nxt, *refs):
    outgoing, incoming, (send, recv) = refs[:N_GROUPS], refs[N_GROUPS:2 * N_GROUPS], refs[2 * N_GROUPS:]
    me = lax.axis_index("blk")
    for one in incoming:
        one[...] = jnp.zeros_like(one)
    barrier = pltpu.get_barrier_semaphore()
    for other in (lax.rem(me + n - 1, n), lax.rem(me + 1, n)):
        pl.semaphore_signal(
            barrier, inc=1, device_id={"blk": other}, device_id_type=pl.DeviceIdType.MESH
        )

    length = u_ref.shape[-1]
    tiles = full.shape[-1] // LANES
    last = tiles - 1
    rem = length - last * LANES
    cut = last * LANES
    lane = lax.broadcasted_iota(jnp.int32, (ROWS, LANES), 1)
    sub = lax.broadcasted_iota(jnp.int32, (ROWS, LANES), 0)
    kv = [kv_ref[l] for l in range(NZ)]

    sides = [(me > 0, me - 1), (me < n - 1, me + 1)]

    def edge_row(i):
        row = (0, ROWS - 1)[i]
        return slice(row, row + 1)

    def grouped(far):
        before = len(GROUPS[0]) * far
        return [(before + k,) + group for k, group in enumerate(GROUPS[far])]

    def copies(far, i):
        return [pltpu.make_async_remote_copy(
            src_ref=outgoing[k].at[i], dst_ref=incoming[k].at[i],
            send_sem=send.at[2 * k + i], recv_sem=recv.at[2 * k + i],
            device_id={"blk": sides[i][1]}, device_id_type=pl.DeviceIdType.MESH,
        ) for k, _, _ in grouped(far)]

    def start(far, source):
        for i in range(2):
            for k, first, number in grouped(far):
                for q in range(number):
                    outgoing[k][i, q:q + 1, :] = source[0, first + q, edge_row(i), :]

            @pl.when(sides[i][0])
            def _():
                for one in copies(far, i):
                    one.start()

    def arrive(far):
        for i in range(2):
            @pl.when(sides[1 - i][0])
            def _():
                for one in copies(far, i):
                    one.wait_recv()

    def spread_out(far, target):
        for i in range(2):
            for k, first, number in grouped(far):
                for q in range(number):
                    target[1, first + q, edge_row(i), :] = incoming[k][i, q:q + 1, :]

    def place(q, value):
        full[0, q, :, 0:cut] = value[:, 0:cut]
        tail = jnp.concatenate(
            [value[:, cut:length], jnp.zeros((ROWS, LANES - rem), jnp.float32)], axis=1
        )
        half = rem + (LANES - rem) // 2
        tail = jnp.where(
            lane < rem,
            tail,
            jnp.where(
                lane < half,
                pltpu.roll(value[:, 0:LANES], rem, 1),
                pltpu.roll(tail, LANES - rem, 1),
            ),
        )
        full[0, q, :, cut:] = tail

    for c in range(2):
        for l in range(NZ):
            place(c * NZ + l, u_ref[c, l])
    place(12, kap_ref[...])
    place(13, wet_ref[...].astype(jnp.float32))
    full[1] = jnp.zeros(full.shape[1:], jnp.float32)
    pl.semaphore_wait(barrier, 2)
    start(0, full)
    closed_step(full, full, mid, kv, lane, sub, tiles)
    start(1, mid)
    mid[1] = jnp.zeros(mid.shape[1:], jnp.float32)
    arrive(0)
    spread_out(0, full)

    def near(t, carry):
        here = columns(t, tiles)[0]
        face = seam_face(
            full[0, 12, :, here], full[0, 13, :, here], full[1, 12, :, here], full[1, 13, :, here], sub
        )
        for q in range(2 * NZ):
            flux = seam_coef(face, q % NZ) * (seam(full[1, q, :, here], sub) - full[0, q, :, here])
            mid[0, q, :, here] = mid[0, q, :, here] + flux
        return carry

    lax.fori_loop(0, tiles, near, 0)
    closed_step(mid, full, nxt, kv, lane, sub, tiles)
    arrive(1)
    spread_out(1, mid)
    for far in range(2):
        for i in range(2):
            @pl.when(sides[i][0])
            def _():
                for one in copies(far, i):
                    one.wait_send()


def step_part(u, kap, wet, kv, n):
    pad = -(-u.shape[-1] // LANES) * LANES
    vmem = pl.BlockSpec(memory_space=pltpu.VMEM)
    smem = pl.BlockSpec(memory_space=pltpu.SMEM)
    return pl.pallas_call(
        functools.partial(step_kernel, n),
        name="two_steps",
        cost_estimate=pl.CostEstimate(flops=20000000, bytes_accessed=12000000, transcendentals=0),
        out_shape=tuple(
            jax.ShapeDtypeStruct(x + (ROWS, pad), jnp.float32) for x in ((2, 14), (2, 12), (1, 12))
        ),
        in_specs=[vmem] * 3 + [smem],
        out_specs=(vmem,) * 3,
        scratch_shapes=[
            pltpu.VMEM((2, number, pad), jnp.float32) for groups in GROUPS for _, number in groups
        ] * 2
        + [pltpu.SemaphoreType.DMA((2 * N_GROUPS,))] * 2,
        compiler_params=pltpu.CompilerParams(
            collective_id=1, has_side_effects=True, vmem_limit_bytes=24 * 2**20
        ),
    )(u, kap, wet, kv)


def local_kernel(
    full, mid, nxt, coup_ref, dest_ref, tile_ref, w_hbm,
    next_ref, sums_ref,
    surf, blocks, acc, weights, w_sem,
):
    length = next_ref.shape[-1]
    count = w_hbm.shape[0]
    tiles = full.shape[-1] // LANES
    last = tiles - 1
    rem = length - last * LANES
    cut = last * LANES
    fetch = pltpu.make_async_copy(w_hbm, weights, w_sem)
    fetch.start()

    sub = lax.broadcasted_iota(jnp.int32, (ROWS, LANES), 0)
    acc[...] = jnp.zeros_like(acc)

    big = ROWS * WIDE
    inner = (FIELDS + 1) * ROWS
    r0 = lax.broadcasted_iota(jnp.int32, (big, FIELDS), 0)
    r1 = lax.broadcasted_iota(jnp.int32, (big, FIELDS), 1)
    pick_f = jnp.where(lax.rem(r0, WIDE) == r1, 1.0, 0.0)
    q0 = lax.broadcasted_iota(jnp.int32, (FIELDS, inner), 0)
    q1 = lax.broadcasted_iota(jnp.int32, (FIELDS, inner), 1)
    pick_q = jnp.where(q1 // ROWS == q0, 1.0, 0.0)
    spread = jnp.dot(
        jnp.dot(pick_f, coup_ref[...], precision=HIGH, preferred_element_type=jnp.float32),
        pick_q, precision=HIGH, preferred_element_type=jnp.float32,
    )
    m0 = lax.broadcasted_iota(jnp.int32, (big, inner), 0)
    m1 = lax.broadcasted_iota(jnp.int32, (big, inner), 1)
    same = (m0 // WIDE) == lax.rem(m1, ROWS)
    sea_entry = (lax.rem(m0, WIDE) == FIELDS) & (m1 // ROWS == FIELDS)
    spread = jnp.where(same, jnp.where(sea_entry, 1.0, spread), 0.0)
    spread_hi, spread_lo = halves(spread)
    spread3 = jnp.concatenate([spread_hi, spread_hi, spread_lo], axis=1)

    def second(t):
        here = columns(t, tiles)[0]
        wet = full[0, 13, :, here]
        face = seam_face(full[0, 12, :, here], wet, full[1, 12, :, here], full[1, 13, :, here], sub)
        new = []
        for q in range(2 * NZ):
            coef = seam_coef(face, q % NZ)
            flux = coef * (seam(full[1, q, :, here], sub) - full[0, q, :, here])
            beyond = seam(mid[1, q, :, here], sub) - flux
            new.append(nxt[0, q, :, here] + coef * (beyond - mid[0, q, :, here]))
        new = [new[:NZ], new[NZ:]]
        sea = jnp.where(wet > 0.0, 1.0, 0.0)
        rows = [new[c][l] * sea for c in range(2) for l in range(NZ)] + [sea]
        return new, here, jnp.concatenate(rows, axis=0)

    def couple(profile):
        hi, lo = halves(profile)
        return jnp.dot(
            spread3, jnp.concatenate([hi, lo, hi], axis=0), preferred_element_type=jnp.float32
        )

    def second_loop(p, carry):
        profiles = []
        for k in range(2):
            new, here, profile = second(2 * p + k)
            profiles.append(profile)
            for c in range(2):
                for l in range(NZ):
                    next_ref[c, l, :, here] = new[c][l]
        here = pl.ds(pl.multiple_of(p * (2 * LANES), LANES), 2 * LANES)
        surf[:, here] = couple(jnp.concatenate(profiles, axis=1))
        return carry

    lax.fori_loop(0, last // 2, second_loop, 0)
    new, here, profile = second(last)
    surf[:, here] = couple(profile)
    for c in range(2):
        for l in range(NZ):
            next_ref[c, l, :, cut:length] = new[c][l][:, 0:rem]

    wlane = lax.broadcasted_iota(jnp.int32, (WIDE, LANES), 1)

    def shifted(j, cur, before):
        shift = rem * j
        if shift == 0:
            return cur
        return pltpu.roll(jnp.where(wlane < LANES - shift, cur, before), shift, 1)

    def align(t, carry):
        here = pl.ds(pl.multiple_of(t * LANES, LANES), LANES)
        prev = pl.ds(pl.multiple_of((t - 1) * LANES, LANES), LANES)
        for j in range(ROWS):
            rows = pl.ds(j * WIDE, WIDE)
            value = shifted(j, surf[rows, here], surf[rows, prev])
            blocks[last * j + t] = value.astype(jnp.bfloat16)
        return carry

    lax.fori_loop(1, last, align, 0, unroll=9)
    for j in range(ROWS + 1):
        if j > 0:
            rows = pl.ds((j - 1) * WIDE, WIDE)
            tail = shifted(j - 1, surf[rows, cut:cut + LANES], surf[rows, cut - LANES:cut])
        if j < ROWS:
            head = surf[pl.ds(j * WIDE, WIDE), 0:LANES]
            if j > 0:
                head = jnp.where(wlane >= rem * j, pltpu.roll(head, rem * j, 1), tail)
        else:
            head = tail
        blocks[last * j] = head.astype(jnp.bfloat16)

    fetch.wait()

    def product(g, carry):
        value = jnp.dot(blocks[g], weights[g], preferred_element_type=jnp.float32)
        seg = dest_ref[g] * NTILE + tile_ref[g]
        here = pl.ds(pl.multiple_of(seg * WIDE, WIDE), WIDE)
        acc[here, :] = acc[here, :] + value
        return carry

    lax.fori_loop(0, count, product, 0, unroll=45)

    owners = sums_ref.shape[0]
    quarter = owners // 4

    def deliver(d, carry):
        slot = lax.rem(d, 4)
        slot = (lax.rem(slot, 2) * 2 + slot // 2) * quarter + d // 4
        for r in range(FIELDS + 1):
            sums_ref[slot, r] = acc[pl.ds(d * (NTILE * WIDE) + r, NTILE, stride=WIDE), :]
        return carry

    lax.fori_loop(0, owners, deliver, 0)


def local_part(full, mid, nxt, coup, dest, tile, weights, length, owners):
    pad = full.shape[-1]
    count = weights.shape[0]
    vmem = pl.BlockSpec(memory_space=pltpu.VMEM)
    smem = pl.BlockSpec(memory_space=pltpu.SMEM)
    return pl.pallas_call(
        local_kernel,
        name="remap",
        cost_estimate=pl.CostEstimate(flops=200000000, bytes_accessed=18000000, transcendentals=0),
        out_shape=(
            jax.ShapeDtypeStruct((2, NZ, ROWS, length), jnp.float32),
            jax.ShapeDtypeStruct((owners, FIELDS + 1, NTILE, AT), jnp.float32),
        ),
        in_specs=[vmem] * 4 + [smem, smem, pl.BlockSpec(memory_space=pl.ANY)],
        out_specs=(vmem, vmem),
        scratch_shapes=[
            pltpu.VMEM((ROWS * WIDE, pad), jnp.float32),
            pltpu.VMEM((count, WIDE, CB), jnp.bfloat16),
            pltpu.VMEM((owners * NTILE * WIDE, AT), jnp.float32),
            pltpu.VMEM(weights.shape, jnp.bfloat16),
            pltpu.SemaphoreType.DMA,
        ],
        compiler_params=pltpu.CompilerParams(vmem_limit_bytes=44 * 2**20),
    )(full, mid, nxt, coup, dest, tile, weights)


PARTS = ((0, 4), (4, 7), (7, 10), (10, 13))


def owner_kernel(n, sums_ref, out_ref, sum1, sum2, got1, got2, got3, ratio, send, recv):
    me = lax.axis_index("blk")
    quarter = n // 4
    core, side, q = lax.rem(me, 2), lax.rem(me // 2, 2), me // 4
    mate1 = me + 1 - 2 * core
    mate2 = me + 2 - 4 * side
    line = [(lax.rem(q + k, quarter)) * 4 + lax.rem(me, 4) for k in range(1, quarter)]

    barrier = pltpu.get_barrier_semaphore()
    for other in [mate1, mate2] + line:
        pl.semaphore_signal(
            barrier, inc=1, device_id={"blk": other}, device_id_type=pl.DeviceIdType.MESH
        )
    pl.semaphore_wait(barrier, 1 + quarter)

    def copy(src, dst, index, other):
        return pltpu.make_async_remote_copy(
            src_ref=src, dst_ref=dst, send_sem=send.at[index], recv_sem=recv.at[index],
            device_id={"blk": other}, device_id_type=pl.DeviceIdType.MESH,
        )

    np_ = len(PARTS)
    ones, twos, threes = [], [], []
    for i, (a, b) in enumerate(PARTS):
        rows = pl.ds(a, b - a)
        ones.append(copy(sums_ref.at[1 - core, :, :, rows], got1.at[:, :, rows], i, mate1))
        ones[-1].start()
    for i, (a, b) in enumerate(PARTS):
        rows = pl.ds(a, b - a)
        ones[i].wait_recv()
        sum1[:, :, rows] = sums_ref[core, :, :, rows] + got1[:, :, rows]
        twos.append(copy(sum1.at[1 - side, :, rows], got2.at[:, rows], np_ + i, mate2))
        twos[-1].start()
    for i, (a, b) in enumerate(PARTS):
        rows = pl.ds(a, b - a)
        twos[i].wait_recv()
        sum2[:, rows] = sum1[side, :, rows] + got2[:, rows]
        threes.append([])
        for k in range(1, quarter):
            to = lax.rem(q + k, quarter)
            threes[i].append(
                copy(sum2.at[to, rows], got3.at[k - 1, rows], 2 * np_ + (k - 1) * np_ + i, line[k - 1])
            )
            threes[i][-1].start()
    total = []
    for i, (a, b) in enumerate(PARTS):
        rows = pl.ds(a, b - a)
        value = sum2[q, rows]
        for k in range(1, quarter):
            threes[i][k - 1].wait_recv()
            value = value + got3[k - 1, rows]
        total.append(value)
    total = jnp.concatenate(total, axis=0)
    below = jnp.maximum(total[FIELDS], 1.0)
    for f in range(FIELDS):
        ratio[f * NTILE:(f + 1) * NTILE, :] = total[f] / below
    for t in range(NTILE):
        out_ref[:, t * AT:(t + 1) * AT] = ratio[pl.ds(t, FIELDS, stride=NTILE), :]
    for group in [ones, twos] + threes:
        for one in group:
            one.wait_send()


def owner_part(sums):
    n = sums.shape[0]
    quarter = n // 4
    block = sums.shape[1:]
    slots = (2 + quarter) * len(PARTS)
    vmem = pl.BlockSpec(memory_space=pltpu.VMEM)
    return pl.pallas_call(
        functools.partial(owner_kernel, n),
        name="owner_sums",
        cost_estimate=pl.CostEstimate(flops=1000000, bytes_accessed=4000000, transcendentals=0),
        out_shape=jax.ShapeDtypeStruct((FIELDS, NTILE * AT), jnp.float32),
        in_specs=[vmem],
        out_specs=vmem,
        scratch_shapes=[
            pltpu.VMEM((2, quarter) + block, jnp.float32),
            pltpu.VMEM((quarter,) + block, jnp.float32),
            pltpu.VMEM((2, quarter) + block, jnp.float32),
            pltpu.VMEM((quarter,) + block, jnp.float32),
            pltpu.VMEM((max(1, quarter - 1),) + block, jnp.float32),
            pltpu.VMEM((FIELDS * NTILE, AT), jnp.float32),
            pltpu.SemaphoreType.DMA((slots,)),
            pltpu.SemaphoreType.DMA((slots,)),
        ],
        compiler_params=pltpu.CompilerParams(
            collective_id=0, has_side_effects=True, vmem_limit_bytes=40 * 2**20
        ),
    )(sums.reshape((2, 2, quarter) + block))


def body(
    ocean_state, kappa_h, kappa_v, wet_depth, coupling, dest_of_block, tile_of_block, remap_weights
):
    size = lax.axis_size("blk")
    steps = step_part(ocean_state, kappa_h, wet_depth, kappa_v, size)
    ocean_next, sums = local_part(
        *steps, coupling, dest_of_block.reshape(-1), tile_of_block, remap_weights,
        ocean_state.shape[-1], size,
    )
    return ocean_next, owner_part(sums)


def solution(mesh):
    return jax.shard_map(
        body,
        mesh=mesh,
        in_specs=(
            P(None, None, ("groups", "blk"), None),
            P("blk", None),
            P(),
            P("blk", None),
            P(),
            P("blk", None),
            P("blk"),
            P("blk", None, None),
        ),
        out_specs=(P(None, None, ("groups", "blk"), None), P(None, ("groups", "blk"))),
        check_vma=False,
    )
```

```python
import functools

import jax
import jax.numpy as jnp
from jax import lax
from jax.experimental import pallas as pl
from jax.experimental.pallas import tpu as pltpu
from jax.sharding import PartitionSpec as P

NZ = 6
FIELDS = 12
CB = 128
AT = 128
NTILE = 8
ROWS = 8
LANES = 128
WIDE = 16
HIGH = lax.Precision.HIGHEST


def lane_pair(cur, before, after, lane):
    east = pltpu.roll(jnp.where(lane == 0, after, cur), LANES - 1, 1)
    west = pltpu.roll(jnp.where(lane == LANES - 1, before, cur), 1, 1)
    return east, west


def row_pair(cur):
    return pltpu.roll(cur, 1, 0), pltpu.roll(cur, ROWS - 1, 0)


def faces(kap, wet, lane, sub, closed):
    nbk = lane_pair(*kap, lane) + row_pair(kap[0])
    nbw = lane_pair(*wet, lane) + row_pair(wet[0])
    depth = [jnp.minimum(wet[0], w) for w in nbw]
    if closed:
        depth[2] = jnp.where(sub == 0, 0.0, depth[2])
        depth[3] = jnp.where(sub == ROWS - 1, 0.0, depth[3])
    return [(jnp.sqrt(kap[0] * k), d) for k, d in zip(nbk, depth)]


def seam_face(kap, wet, halo_kap, halo_wet, sub):
    edge = (sub == 0) | (sub == ROWS - 1)
    root = jnp.sqrt(kap * seam(halo_kap, sub))
    return root, jnp.where(edge, jnp.minimum(wet, seam(halo_wet, sub)), 0.0)


def seam(halo, sub):
    up, down = row_pair(halo)
    return jnp.where(sub == 0, up, down)


def halves(x):
    hi = x.astype(jnp.bfloat16)
    return hi, (x - hi.astype(jnp.float32)).astype(jnp.bfloat16)


def mixed(tiles, face, wet, kv):
    out = [[None] * NZ for _ in range(2)]
    for l in range(NZ):
        coef = [jnp.where(l < depth, root, 0.0) for root, depth in face]
        below = jnp.where(l + 1 < wet, kv[l], 0.0) if l + 1 < NZ else None
        above = jnp.where(l < wet, kv[l - 1], 0.0) if l > 0 else None
        for c in range(2):
            cur = tiles[c][l][0]
            change = coef[0] * (tiles[c][l][1] - cur)
            for a, v in zip(coef[1:], tiles[c][l][2:]):
                change = change + a * (v - cur)
            if below is not None:
                change = change + below * (tiles[c][l + 1][0] - cur)
            if above is not None:
                change = change + above * (tiles[c][l - 1][0] - cur)
            out[c][l] = cur + change
    return out


def columns(t, tiles):
    def at(i):
        return pl.ds(pl.multiple_of(i * LANES, LANES), LANES)

    return [at(t), at(lax.rem(t + tiles - 1, tiles)), at(lax.rem(t + 1, tiles))]


def closed_step(src, full, dst, kv, lane, sub, tiles):
    def one(t, carry):
        cols = columns(t, tiles)
        get = lambda ref, q: [ref[0, q, :, s] for s in cols]
        state = []
        for c in range(2):
            state.append([])
            for l in range(NZ):
                cur = get(src, c * NZ + l)
                state[c].append((cur[0],) + lane_pair(*cur, lane) + row_pair(cur[0]))
        wet = get(full, 12 + 1)
        face = faces(get(full, 12), wet, lane, sub, True)
        new = mixed(state, face, wet[0], kv)
        for c in range(2):
            for l in range(NZ):
                dst[0, c * NZ + l, :, cols[0]] = new[c][l]
        return carry

    lax.fori_loop(0, tiles, one, 0)


def seam_coef(face, l):
    return jnp.where(l < face[1], face[0], 0.0)


GROUPS = (((0, 8), (8, 4), (12, 2)), ((0, 8), (8, 4)))
N_GROUPS = sum(len(groups) for groups in GROUPS)


def step_kernel(n, u_ref, kap_ref, wet_ref, kv_ref, full, mid, nxt, *refs):
    outgoing, incoming, (send, recv) = refs[:N_GROUPS], refs[N_GROUPS:2 * N_GROUPS], refs[2 * N_GROUPS:]
    me = lax.axis_index("blk")
    for one in incoming:
        one[...] = jnp.zeros_like(one)
    barrier = pltpu.get_barrier_semaphore()
    for other in (lax.rem(me + n - 1, n), lax.rem(me + 1, n)):
        pl.semaphore_signal(
            barrier, inc=1, device_id={"blk": other}, device_id_type=pl.DeviceIdType.MESH
        )

    length = u_ref.shape[-1]
    tiles = full.shape[-1] // LANES
    last = tiles - 1
    rem = length - last * LANES
    cut = last * LANES
    lane = lax.broadcasted_iota(jnp.int32, (ROWS, LANES), 1)
    sub = lax.broadcasted_iota(jnp.int32, (ROWS, LANES), 0)
    kv = [kv_ref[l] for l in range(NZ)]

    sides = [(me > 0, me - 1), (me < n - 1, me + 1)]

    def edge_row(i):
        row = (0, ROWS - 1)[i]
        return slice(row, row + 1)

    def grouped(far):
        before = len(GROUPS[0]) * far
        return [(before + k,) + group for k, group in enumerate(GROUPS[far])]

    def copies(far, i):
        return [pltpu.make_async_remote_copy(
            src_ref=outgoing[k].at[i], dst_ref=incoming[k].at[i],
            send_sem=send.at[2 * k + i], recv_sem=recv.at[2 * k + i],
            device_id={"blk": sides[i][1]}, device_id_type=pl.DeviceIdType.MESH,
        ) for k, _, _ in grouped(far)]

    def start(far, source):
        for i in range(2):
            for k, first, number in grouped(far):
                for q in range(number):
                    outgoing[k][i, q:q + 1, :] = source[0, first + q, edge_row(i), :]

            @pl.when(sides[i][0])
            def _():
                for one in copies(far, i):
                    one.start()

    def arrive(far):
        for i in range(2):
            @pl.when(sides[1 - i][0])
            def _():
                for one in copies(far, i):
                    one.wait_recv()

    def spread_out(far, target):
        for i in range(2):
            for k, first, number in grouped(far):
                for q in range(number):
                    target[1, first + q, edge_row(i), :] = incoming[k][i, q:q + 1, :]

    def place(q, value):
        full[0, q, :, 0:cut] = value[:, 0:cut]
        tail = jnp.concatenate(
            [value[:, cut:length], jnp.zeros((ROWS, LANES - rem), jnp.float32)], axis=1
        )
        half = rem + (LANES - rem) // 2
        tail = jnp.where(
            lane < rem,
            tail,
            jnp.where(
                lane < half,
                pltpu.roll(value[:, 0:LANES], rem, 1),
                pltpu.roll(tail, LANES - rem, 1),
            ),
        )
        full[0, q, :, cut:] = tail

    for c in range(2):
        for l in range(NZ):
            place(c * NZ + l, u_ref[c, l])
    place(12, kap_ref[...])
    place(13, wet_ref[...].astype(jnp.float32))
    full[1] = jnp.zeros(full.shape[1:], jnp.float32)
    pl.semaphore_wait(barrier, 2)
    start(0, full)
    closed_step(full, full, mid, kv, lane, sub, tiles)
    start(1, mid)
    mid[1] = jnp.zeros(mid.shape[1:], jnp.float32)
    arrive(0)
    spread_out(0, full)

    def near(t, carry):
        here = columns(t, tiles)[0]
        face = seam_face(
            full[0, 12, :, here], full[0, 13, :, here], full[1, 12, :, here], full[1, 13, :, here], sub
        )
        for q in range(2 * NZ):
            flux = seam_coef(face, q % NZ) * (seam(full[1, q, :, here], sub) - full[0, q, :, here])
            mid[0, q, :, here] = mid[0, q, :, here] + flux
        return carry

    lax.fori_loop(0, tiles, near, 0)
    closed_step(mid, full, nxt, kv, lane, sub, tiles)
    arrive(1)
    spread_out(1, mid)
    for far in range(2):
        for i in range(2):
            @pl.when(sides[i][0])
            def _():
                for one in copies(far, i):
                    one.wait_send()


def step_part(u, kap, wet, kv, n):
    pad = -(-u.shape[-1] // LANES) * LANES
    vmem = pl.BlockSpec(memory_space=pltpu.VMEM)
    smem = pl.BlockSpec(memory_space=pltpu.SMEM)
    return pl.pallas_call(
        functools.partial(step_kernel, n),
        name="two_steps",
        cost_estimate=pl.CostEstimate(flops=20000000, bytes_accessed=12000000, transcendentals=0),
        out_shape=tuple(
            jax.ShapeDtypeStruct(x + (ROWS, pad), jnp.float32) for x in ((2, 14), (2, 12), (1, 12))
        ),
        in_specs=[vmem] * 3 + [smem],
        out_specs=(vmem,) * 3,
        scratch_shapes=[
            pltpu.VMEM((2, number, pad), jnp.float32) for groups in GROUPS for _, number in groups
        ] * 2
        + [pltpu.SemaphoreType.DMA((2 * N_GROUPS,))] * 2,
        compiler_params=pltpu.CompilerParams(
            collective_id=1, has_side_effects=True, vmem_limit_bytes=24 * 2**20
        ),
    )(u, kap, wet, kv)


def local_kernel(
    full, mid, nxt, coup_ref, seg_ref, w_hbm,
    next_ref, sums_ref,
    surf, blocks, acc, weights, w_sem,
):
    length = next_ref.shape[-1]
    count = w_hbm.shape[0]
    tiles = full.shape[-1] // LANES
    last = tiles - 1
    rem = length - last * LANES
    cut = last * LANES
    fetch = pltpu.make_async_copy(w_hbm, weights, w_sem)
    fetch.start()

    sub = lax.broadcasted_iota(jnp.int32, (ROWS, LANES), 0)
    acc[...] = jnp.zeros_like(acc)

    big = ROWS * WIDE
    inner = (FIELDS + 1) * ROWS
    r0 = lax.broadcasted_iota(jnp.int32, (big, FIELDS), 0)
    r1 = lax.broadcasted_iota(jnp.int32, (big, FIELDS), 1)
    pick_f = jnp.where(lax.rem(r0, WIDE) == r1, 1.0, 0.0)
    q0 = lax.broadcasted_iota(jnp.int32, (FIELDS, inner), 0)
    q1 = lax.broadcasted_iota(jnp.int32, (FIELDS, inner), 1)
    pick_q = jnp.where(q1 // ROWS == q0, 1.0, 0.0)
    spread = jnp.dot(
        jnp.dot(pick_f, coup_ref[...], precision=HIGH, preferred_element_type=jnp.float32),
        pick_q, precision=HIGH, preferred_element_type=jnp.float32,
    )
    m0 = lax.broadcasted_iota(jnp.int32, (big, inner), 0)
    m1 = lax.broadcasted_iota(jnp.int32, (big, inner), 1)
    same = (m0 // WIDE) == lax.rem(m1, ROWS)
    sea_entry = (lax.rem(m0, WIDE) == FIELDS) & (m1 // ROWS == FIELDS)
    spread = jnp.where(same, jnp.where(sea_entry, 1.0, spread), 0.0)
    spread_hi, spread_lo = halves(spread)
    spread3 = jnp.concatenate([spread_hi, spread_hi, spread_lo], axis=1)

    def second(t):
        here = columns(t, tiles)[0]
        wet = full[0, 13, :, here]
        face = seam_face(full[0, 12, :, here], wet, full[1, 12, :, here], full[1, 13, :, here], sub)
        new = []
        for q in range(2 * NZ):
            coef = seam_coef(face, q % NZ)
            flux = coef * (seam(full[1, q, :, here], sub) - full[0, q, :, here])
            beyond = seam(mid[1, q, :, here], sub) - flux
            new.append(nxt[0, q, :, here] + coef * (beyond - mid[0, q, :, here]))
        new = [new[:NZ], new[NZ:]]
        sea = jnp.where(wet > 0.0, 1.0, 0.0)
        rows = [new[c][l] * sea for c in range(2) for l in range(NZ)] + [sea]
        return new, here, jnp.concatenate(rows, axis=0)

    def couple(profile):
        hi, lo = halves(profile)
        return jnp.dot(
            spread3, jnp.concatenate([hi, lo, hi], axis=0), preferred_element_type=jnp.float32
        )

    def second_loop(p, carry):
        profiles = []
        for k in range(2):
            new, here, profile = second(2 * p + k)
            profiles.append(profile)
            for c in range(2):
                for l in range(NZ):
                    next_ref[c, l, :, here] = new[c][l]
        here = pl.ds(pl.multiple_of(p * (2 * LANES), LANES), 2 * LANES)
        surf[:, here] = couple(jnp.concatenate(profiles, axis=1))
        return carry

    lax.fori_loop(0, last // 2, second_loop, 0)
    new, here, profile = second(last)
    surf[:, here] = couple(profile)
    for c in range(2):
        for l in range(NZ):
            next_ref[c, l, :, cut:length] = new[c][l][:, 0:rem]

    wlane = lax.broadcasted_iota(jnp.int32, (WIDE, LANES), 1)

    def shifted(j, cur, before):
        shift = rem * j
        if shift == 0:
            return cur
        return pltpu.roll(jnp.where(wlane < LANES - shift, cur, before), shift, 1)

    def align(t, carry):
        here = pl.ds(pl.multiple_of(t * LANES, LANES), LANES)
        prev = pl.ds(pl.multiple_of((t - 1) * LANES, LANES), LANES)
        for j in range(ROWS):
            rows = pl.ds(j * WIDE, WIDE)
            value = shifted(j, surf[rows, here], surf[rows, prev])
            blocks[last * j + t] = value.astype(jnp.bfloat16)
        return carry

    lax.fori_loop(1, last, align, 0, unroll=9)
    for j in range(ROWS + 1):
        if j > 0:
            rows = pl.ds((j - 1) * WIDE, WIDE)
            tail = shifted(j - 1, surf[rows, cut:cut + LANES], surf[rows, cut - LANES:cut])
        if j < ROWS:
            head = surf[pl.ds(j * WIDE, WIDE), 0:LANES]
            if j > 0:
                head = jnp.where(wlane >= rem * j, pltpu.roll(head, rem * j, 1), tail)
        else:
            head = tail
        blocks[last * j] = head.astype(jnp.bfloat16)

    fetch.wait()

    def product(g, carry):
        value = jnp.dot(blocks[g], weights[g], preferred_element_type=jnp.float32)
        seg = seg_ref[g]
        here = pl.ds(pl.multiple_of(seg * WIDE, WIDE), WIDE)
        acc[here, :] = acc[here, :] + value
        return carry

    lax.fori_loop(0, count, product, 0, unroll=45)

    owners = sums_ref.shape[0]
    quarter = owners // 4

    def deliver(d, carry):
        slot = lax.rem(d, 4)
        slot = (lax.rem(slot, 2) * 2 + slot // 2) * quarter + d // 4
        for r in range(FIELDS + 1):
            sums_ref[slot, r] = acc[pl.ds(d * (NTILE * WIDE) + r, NTILE, stride=WIDE), :]
        return carry

    lax.fori_loop(0, owners, deliver, 0)


def local_part(full, mid, nxt, coup, seg, weights, length, owners):
    pad = full.shape[-1]
    count = weights.shape[0]
    vmem = pl.BlockSpec(memory_space=pltpu.VMEM)
    smem = pl.BlockSpec(memory_space=pltpu.SMEM)
    return pl.pallas_call(
        local_kernel,
        name="remap",
        cost_estimate=pl.CostEstimate(flops=200000000, bytes_accessed=18000000, transcendentals=0),
        out_shape=(
            jax.ShapeDtypeStruct((2, NZ, ROWS, length), jnp.float32),
            jax.ShapeDtypeStruct((owners, FIELDS + 1, NTILE, AT), jnp.float32),
        ),
        in_specs=[vmem] * 4 + [smem, pl.BlockSpec(memory_space=pl.ANY)],
        out_specs=(vmem, vmem),
        scratch_shapes=[
            pltpu.VMEM((ROWS * WIDE, pad), jnp.float32),
            pltpu.VMEM((count, WIDE, CB), jnp.bfloat16),
            pltpu.VMEM((owners * NTILE * WIDE, AT), jnp.float32),
            pltpu.VMEM(weights.shape, jnp.bfloat16),
            pltpu.SemaphoreType.DMA,
        ],
        compiler_params=pltpu.CompilerParams(vmem_limit_bytes=44 * 2**20),
    )(full, mid, nxt, coup, seg, weights)


PARTS = ((0, 4), (4, 7), (7, 10), (10, 13))


def owner_kernel(n, sums_ref, out_ref, sum1, sum2, got1, got2, got3, ratio, send, recv):
    me = lax.axis_index("blk")
    quarter = n // 4
    core, side, q = lax.rem(me, 2), lax.rem(me // 2, 2), me // 4
    mate1 = me + 1 - 2 * core
    mate2 = me + 2 - 4 * side
    line = [(lax.rem(q + k, quarter)) * 4 + lax.rem(me, 4) for k in range(1, quarter)]

    barrier = pltpu.get_barrier_semaphore()
    for other in [mate1, mate2] + line:
        pl.semaphore_signal(
            barrier, inc=1, device_id={"blk": other}, device_id_type=pl.DeviceIdType.MESH
        )
    pl.semaphore_wait(barrier, 1 + quarter)

    def copy(src, dst, index, other):
        return pltpu.make_async_remote_copy(
            src_ref=src, dst_ref=dst, send_sem=send.at[index], recv_sem=recv.at[index],
            device_id={"blk": other}, device_id_type=pl.DeviceIdType.MESH,
        )

    np_ = len(PARTS)
    ones, twos, threes = [], [], []
    for i, (a, b) in enumerate(PARTS):
        rows = pl.ds(a, b - a)
        ones.append(copy(sums_ref.at[1 - core, :, :, rows], got1.at[:, :, rows], i, mate1))
        ones[-1].start()
    for i, (a, b) in enumerate(PARTS):
        rows = pl.ds(a, b - a)
        ones[i].wait_recv()
        sum1[:, :, rows] = sums_ref[core, :, :, rows] + got1[:, :, rows]
        twos.append(copy(sum1.at[1 - side, :, rows], got2.at[:, rows], np_ + i, mate2))
        twos[-1].start()
    for i, (a, b) in enumerate(PARTS):
        rows = pl.ds(a, b - a)
        twos[i].wait_recv()
        sum2[:, rows] = sum1[side, :, rows] + got2[:, rows]
        threes.append([])
        for k in range(1, quarter):
            to = lax.rem(q + k, quarter)
            threes[i].append(
                copy(sum2.at[to, rows], got3.at[k - 1, rows], 2 * np_ + (k - 1) * np_ + i, line[k - 1])
            )
            threes[i][-1].start()
    total = []
    for i, (a, b) in enumerate(PARTS):
        rows = pl.ds(a, b - a)
        value = sum2[q, rows]
        for k in range(1, quarter):
            threes[i][k - 1].wait_recv()
            value = value + got3[k - 1, rows]
        total.append(value)
    total = jnp.concatenate(total, axis=0)
    below = jnp.maximum(total[FIELDS], 1.0)
    for f in range(FIELDS):
        ratio[f * NTILE:(f + 1) * NTILE, :] = total[f] / below
    for t in range(NTILE):
        out_ref[:, t * AT:(t + 1) * AT] = ratio[pl.ds(t, FIELDS, stride=NTILE), :]
    for group in [ones, twos] + threes:
        for one in group:
            one.wait_send()


def owner_part(sums):
    n = sums.shape[0]
    quarter = n // 4
    block = sums.shape[1:]
    slots = (2 + quarter) * len(PARTS)
    vmem = pl.BlockSpec(memory_space=pltpu.VMEM)
    return pl.pallas_call(
        functools.partial(owner_kernel, n),
        name="owner_sums",
        cost_estimate=pl.CostEstimate(flops=1000000, bytes_accessed=4000000, transcendentals=0),
        out_shape=jax.ShapeDtypeStruct((FIELDS, NTILE * AT), jnp.float32),
        in_specs=[vmem],
        out_specs=vmem,
        scratch_shapes=[
            pltpu.VMEM((2, quarter) + block, jnp.float32),
            pltpu.VMEM((quarter,) + block, jnp.float32),
            pltpu.VMEM((2, quarter) + block, jnp.float32),
            pltpu.VMEM((quarter,) + block, jnp.float32),
            pltpu.VMEM((max(1, quarter - 1),) + block, jnp.float32),
            pltpu.VMEM((FIELDS * NTILE, AT), jnp.float32),
            pltpu.SemaphoreType.DMA((slots,)),
            pltpu.SemaphoreType.DMA((slots,)),
        ],
        compiler_params=pltpu.CompilerParams(
            collective_id=0, has_side_effects=True, vmem_limit_bytes=40 * 2**20
        ),
    )(sums.reshape((2, 2, quarter) + block))


def body(
    ocean_state, kappa_h, kappa_v, wet_depth, coupling, dest_of_block, tile_of_block, remap_weights
):
    size = lax.axis_size("blk")
    steps = step_part(ocean_state, kappa_h, wet_depth, kappa_v, size)
    ocean_next, sums = local_part(
        *steps, coupling, dest_of_block.reshape(-1) * NTILE + tile_of_block, remap_weights,
        ocean_state.shape[-1], size,
    )
    return ocean_next, owner_part(sums)


def solution(mesh):
    return jax.shard_map(
        body,
        mesh=mesh,
        in_specs=(
            P(None, None, ("groups", "blk"), None),
            P("blk", None),
            P(),
            P("blk", None),
            P(),
            P("blk", None),
            P("blk"),
            P("blk", None, None),
        ),
        out_specs=(P(None, None, ("groups", "blk"), None), P(None, ("groups", "blk"))),
        check_vma=False,
    )
```
